256 devices in a mesh: seq: 64 (over x, z, y_lo), head: 4 (over y_hi, core).
Axes of the slice: x: 4, y: 4 (y_hi: 2, y_lo: 2; y = y_hi * 2 + y_lo), z: 8, core: 2. Of those that a mesh axis runs over, the one named last changes fastest.
Arguments:
- query_nope: bfloat16 [8192, 8192], P('seq', 'head'), may hold values from -6 to 6
- query_rope: bfloat16 [8192, 4096], P('seq', 'head'), may hold values from -6 to 6
- latent: bfloat16 [8192, 512], P('seq'), may hold values from -6 to 6
- key_rope: bfloat16 [8192, 64], P('seq'), may hold values from -6 to 6
- up_key: bfloat16 [512, 8192], P(None, 'head'), may hold values from -0.25 to 0.25
- up_value: bfloat16 [512, 8192], P(None, 'head'), may hold values from -0.25 to 0.25
- grad_out: bfloat16 [8192, 8192], P('seq', 'head'), may hold values from -6 to 6
- group_order: int32 [128], replicated, may hold values from 0 to 127, as said below
- tile_mask: int32 [128, 128], replicated, may hold values from 0 to 1, as said below
Outputs:
- output: bfloat16 [8192, 8192], P('seq', 'head')
- grad_query_nope: bfloat16 [8192, 8192], P('seq', 'head')
- grad_query_rope: bfloat16 [8192, 4096], P('seq', 'head')
- grad_latent: bfloat16 [8192, 512], P('seq')
- grad_key_rope: bfloat16 [8192, 64], P('seq')
The draws below stay inside these ranges and needn't reach their ends.
Inputs may be any that keep to these rules, and one draw needn't show every extreme that they name: `group_order`: entries 2 d and 2 d + 1 name the groups of device d of seq, whose rows hold them in that order; the first is under 128 / 2 and the second is 127 minus the first; every group appears once. `tile_mask`: entry [a, b] is 1 exactly where group b does not come after group a and both lie in the same document; documents are runs of 1 to 8 consecutive groups, and the first document has exactly 8.
All inputs are finite; a program needn't handle non-finite values.
Results may differ from the reference program's by a relative error of at most 0.028.
Values may be sent and summed in bfloat16 or wider, within the bound.
A program may use at most 128 MiB of HBM per device.

```python
import jax
import jax.numpy as jnp
from jax import lax

TOK_DEV = 128
LATENT = 512
ROPE = 64
NOPE = 128
DOC_GROUPS = 8
TOKENS = 8192
HEADS = 64
GROUPS = 128


def draw_key_rope(key, part):
    key = jax.random.fold_in(key, 11)
    first_key = jax.random.fold_in(key, 0)
    values = jnp.clip(jax.random.normal(first_key, (TOKENS, ROPE), jnp.float32), -6.0, 6.0)
    return values.astype(jnp.bfloat16)


def draw_query_rope(key, part):
    key = jax.random.fold_in(key, 13)
    first_key = jax.random.fold_in(key, 0)
    values = jnp.clip(jax.random.normal(first_key, (TOKENS, HEADS, ROPE), jnp.float32), -6.0, 6.0)
    return values.reshape(TOKENS, HEADS * ROPE).astype(jnp.bfloat16)


def draw_group_order(key, part):
    key = jax.random.fold_in(key, 3)
    lower = jax.random.permutation(key, GROUPS // 2).astype(jnp.int32)
    return jnp.stack([lower, GROUPS - 1 - lower], 1).reshape(GROUPS)


def draw_tile_mask(key, part):
    key = jax.random.fold_in(key, 5)
    group_ids = jnp.arange(GROUPS, dtype=jnp.int32)
    lengths = jax.random.randint(key, (GROUPS,), 1, DOC_GROUPS + 1).astype(jnp.int32)
    lengths = jnp.where(group_ids == 0, DOC_GROUPS, lengths)
    ends = jnp.cumsum(lengths)
    begins = ends - lengths
    flags = jnp.sum((begins[None, :] == group_ids[:, None]).astype(jnp.int32), axis=1)
    document = jnp.cumsum(flags)
    same = document[:, None] == document[None, :]
    return (same & (group_ids[None, :] <= group_ids[:, None])).astype(jnp.int32)


def block_scale(own_key, dims, pieces, smallest, high):
    gain = 1.0
    for dim, blocks in pieces:
        draws = jax.random.uniform(jax.random.fold_in(jax.random.fold_in(own_key, 6), dim), (blocks,), jnp.float32, smallest / len(pieces), high / len(pieces))
        gain = gain * jnp.repeat(jnp.exp(draws), dims[dim] // blocks).reshape((-1,) + (1,) * (len(dims) - 1 - dim))
    return gain


def bell_draw(stream_key, extent, spread, reach, cuts=(), kind=jnp.bfloat16):
    result = jax.random.normal(stream_key, extent, jnp.float32) * spread
    if len(cuts) > 0:
        result = block_scale(stream_key, extent, cuts, -0.22, 0.18) * result
    return jnp.clip(result, min=-reach, max=reach).astype(kind)


def setup_inputs(seed: int = 0) -> dict:
    keys = jax.random.split(jax.random.key(seed), 10)
    return {
        "query_nope": bell_draw(keys[0], (TOKENS, HEADS * NOPE), 1.0, 6.0, ((0, 64), (1, 4))),
        "query_rope": draw_query_rope(jax.random.fold_in(keys[9], 71), 0),
        "latent": bell_draw(keys[2], (TOKENS, LATENT), 1.0, 6.0, ((0, 64),)),
        "key_rope": draw_key_rope(jax.random.fold_in(keys[9], 71), 0),
        "up_key": bell_draw(keys[4], (LATENT, HEADS * NOPE), LATENT ** -0.5, 0.25, ((1, 4),)),
        "up_value": bell_draw(keys[5], (LATENT, HEADS * NOPE), LATENT ** -0.5, 0.25, ((1, 4),)),
        "grad_out": bell_draw(keys[6], (TOKENS, HEADS * NOPE), 1.0, 6.0, ((0, 64), (1, 4))),
        "group_order": draw_group_order(jax.random.fold_in(keys[9], 71), 0),
        "tile_mask": draw_tile_mask(jax.random.fold_in(keys[9], 71), 0),
    }


def reference(query_nope, query_rope, latent, key_rope, up_key, up_value, grad_out, group_order, tile_mask):
    all_rows = latent.shape[0]
    group_rows = TOK_DEV // 2
    width = LATENT + ROPE
    span = DOC_GROUPS
    score_scale = (NOPE + ROPE) ** -0.5
    blocks = jnp.arange(GROUPS, dtype=jnp.int32)
    slot_of = jnp.sum(jnp.where(group_order[:, None] == blocks[None, :], blocks[:, None], 0), axis=0).astype(jnp.int32)

    def by_position(array, inner):
        return jnp.take(array.reshape((GROUPS, group_rows) + inner), slot_of, axis=0)

    key_rows = jnp.concatenate([latent, key_rope], 1)
    keys_pos = by_position(key_rows, (width,))
    keys_pad = jnp.concatenate([jnp.zeros((span - 1, group_rows, width), jnp.bfloat16), keys_pos], 0)
    nope_pos = by_position(query_nope, (HEADS, NOPE))
    rope_pos = by_position(query_rope, (HEADS, ROPE))
    grad_pos = by_position(grad_out, (HEADS, NOPE))
    weight_key = up_key.reshape(LATENT, HEADS, NOPE).astype(jnp.float32)
    weight_value = up_value.reshape(LATENT, HEADS, NOPE).astype(jnp.float32)
    offsets = jnp.arange(group_rows, dtype=jnp.int32)
    window_index = jnp.arange(span, dtype=jnp.int32)
    key_offset = jnp.tile(offsets, span)
    key_slot = jnp.repeat(window_index, group_rows, total_repeat_length=span * group_rows)

    def one_group(running, index):
        group_id = index.astype(jnp.int32)
        window = lax.dynamic_slice_in_dim(keys_pad, group_id, span, 0).reshape(span * group_rows, width)
        latent_win = window[:, :LATENT]
        near = group_id - (span - 1) + window_index
        tile_row = lax.dynamic_index_in_dim(tile_mask, group_id, 0, keepdims=False)
        picked = jnp.sum(jnp.where(blocks[None, :] == jnp.maximum(near, 0)[:, None], tile_row[None, :], 0), axis=1)
        live = (near >= 0) & (picked == 1)
        live_keys = jnp.repeat(live, group_rows, total_repeat_length=span * group_rows)
        causal = (key_slot[None, :] < span - 1) | (key_offset[None, :] <= offsets[:, None])
        allowed = (live_keys[None, :] & causal)[None, :, :]
        query_part = lax.dynamic_index_in_dim(nope_pos, group_id, 0, keepdims=False)
        rope_part = lax.dynamic_index_in_dim(rope_pos, group_id, 0, keepdims=False)
        grad_part = lax.dynamic_index_in_dim(grad_pos, group_id, 0, keepdims=False)
        query_lat = jnp.einsum("thd,chd->thc", query_part.astype(jnp.float32), weight_key).astype(jnp.bfloat16)
        query_full = jnp.concatenate([query_lat, rope_part], 2)
        scores = jnp.einsum("thf,kf->htk", query_full.astype(jnp.float32), window.astype(jnp.float32)) * score_scale
        row_top = jnp.max(jnp.where(allowed, scores, -1e30), axis=2, keepdims=True)
        weights = jnp.where(allowed, jnp.exp(scores - row_top), 0.0)
        normed = weights / jnp.sum(weights, axis=2, keepdims=True)
        normed_low = normed.astype(jnp.bfloat16)
        output_lat = jnp.einsum("htk,kc->htc", normed_low.astype(jnp.float32), latent_win.astype(jnp.float32))
        output_head = jnp.einsum("htc,chd->thd", output_lat.astype(jnp.bfloat16).astype(jnp.float32), weight_value).astype(jnp.bfloat16)
        grad_lat = jnp.einsum("thd,chd->htc", grad_part.astype(jnp.float32), weight_value)
        grad_lat_low = grad_lat.astype(jnp.bfloat16)
        row_delta = jnp.sum(grad_lat * output_lat, axis=2, keepdims=True)
        grad_prob = jnp.einsum("htc,kc->htk", grad_lat_low.astype(jnp.float32), latent_win.astype(jnp.float32))
        grad_score = (normed * (grad_prob - row_delta)).astype(jnp.bfloat16)
        grad_query = jnp.einsum("htk,kf->htf", grad_score.astype(jnp.float32), window.astype(jnp.float32)) * score_scale
        grad_nope = jnp.einsum("htc,chd->thd", grad_query[:, :, :LATENT].astype(jnp.bfloat16).astype(jnp.float32), weight_key).astype(jnp.bfloat16)
        grad_rope = grad_query[:, :, LATENT:].astype(jnp.bfloat16).transpose(1, 0, 2)
        score_term = jnp.einsum("htk,thf->kf", grad_score.astype(jnp.float32), query_full.astype(jnp.float32)) * score_scale
        value_term = jnp.einsum("htk,htc->kc", normed_low.astype(jnp.float32), grad_lat_low.astype(jnp.float32))
        term = (score_term + jnp.pad(value_term, ((0, 0), (0, ROPE)))).reshape(span, group_rows, width)
        updated = lax.dynamic_slice_in_dim(running, group_id, span, 0) + term
        running = lax.dynamic_update_slice_in_dim(running, updated, group_id, 0)
        return running, (output_head.reshape(group_rows, HEADS * NOPE), grad_nope.reshape(group_rows, HEADS * NOPE), grad_rope.reshape(group_rows, HEADS * ROPE))

    start_sum = jnp.zeros((GROUPS + span - 1, group_rows, width), jnp.float32)
    grad_pad, stacked = lax.scan(one_group, start_sum, jnp.arange(GROUPS, dtype=jnp.int32))
    output_pos, nope_pos_grad, rope_pos_grad = stacked

    def by_rows(array):
        return jnp.take(array, group_order, axis=0).reshape((all_rows,) + array.shape[2:])

    output = by_rows(output_pos)
    grad_query_nope = by_rows(nope_pos_grad)
    grad_query_rope = by_rows(rope_pos_grad)
    grad_keys = by_rows(grad_pad[span - 1:])
    grad_latent = grad_keys[:, :LATENT].astype(jnp.bfloat16)
    grad_key_rope = grad_keys[:, LATENT:].astype(jnp.bfloat16)
    return (output, grad_query_nope, grad_query_rope, grad_latent, grad_key_rope)
```

```python
import functools
import math

import jax
import jax.numpy as jnp
from jax import lax
from jax.experimental import pallas as pl
from jax.experimental.pallas import tpu as pltpu
from jax.sharding import PartitionSpec as P

HEAD_DEV = 16
LATENT = 512
ROPE = 64
NOPE = 128
SPAN = 8
GROUP = 64
PAD = 128
WIDTH = PAD + LATENT
KEYS = SPAN * GROUP
ROWS = HEAD_DEV * GROUP
MESH = pl.DeviceIdType.MESH
SCALE = (NOPE + ROPE) ** (-0.5)
SCALE2 = SCALE * math.log2(math.e)
BLOCK = 256
F32 = jnp.float32
BF16 = jnp.bfloat16


def dot_nt(a, b):
    return lax.dot_general(a, b, (((1,), (1,)), ((), ())), preferred_element_type=F32)


def dot_nn(a, b):
    return lax.dot_general(a, b, (((1,), (0,)), ((), ())), preferred_element_type=F32)


def dot_tn(a, b):
    return lax.dot_general(a, b, (((0,), (0,)), ((), ())), preferred_element_type=F32)


def kernel(
    qn_hbm, qr_hbm, lat_ref, rope_ref, uk_hbm, uv_hbm, go_hbm, order_sm, order_row, mask_ref,
    out_hbm, gqn_hbm, gqr_hbm, glat_ref, grope_ref,
    qn, qr, uk, uv, gout, out_v, gqn_v, gqr_v,
    keyf, xbuf, send1, recv1, gather2, onehot, send2, window,
    qfull, glow, olat, gqlat, probs, dscore, bias,
    dwin, dsend, dpair, dmine, recvb, asum, apair, bsum, bpair, send4, recv4,
    insem, outsem, s1, s1x, r1, s1c, r1c, s2, s2x, r2, s2c, r2c,
    s3c, r3c, s4, s4x, r4, s5, r5, s6, r6, s7, s7x, r7, s7c, r7c,
):
    seq = lax.axis_index("seq")
    head = lax.axis_index("head")
    core = lax.rem(head, 2)
    parity = lax.rem(seq + core, 2)
    other = 1 - parity
    place = lax.div(seq, 2)
    half = lax.div(seq, 32)
    pair = lax.div(lax.rem(seq, 32), 2)
    seq_par = lax.rem(seq, 2)
    twin = (seq, head + 1 - 2 * core)
    far = (seq, lax.rem(head + 2, 4))

    def peer(o):
        return (2 * o + parity, head)

    loads = [
        pltpu.make_async_copy(src, dst, insem.at[n])
        for n, (src, dst) in enumerate(
            [(qn_hbm, qn), (qr_hbm, qr), (uk_hbm, uk), (uv_hbm, uv), (go_hbm, gout)]
        )
    ]
    for load in loads:
        load.start()

    barrier = pltpu.get_barrier_semaphore()

    def greet(i, carry):
        o = lax.rem(place + i, 32)
        pl.semaphore_signal(barrier, inc=1, device_id=peer(o), device_id_type=MESH)
        return carry

    lax.fori_loop(1, 32, greet, 0)

    @pl.when(core == 1)
    def _():
        pl.semaphore_signal(barrier, inc=1, device_id=peer(place), device_id_type=MESH)

    pl.semaphore_signal(barrier, inc=1, device_id=twin, device_id_type=MESH)
    pl.semaphore_signal(barrier, inc=1, device_id=far, device_id_type=MESH)

    lanes = lax.broadcasted_iota(jnp.int32, (128, PAD), 1)
    for b in range(4):
        keyf[b + 1] = lat_ref[:, b * 128:(b + 1) * 128].astype(F32)
    keyf[0] = jnp.concatenate([rope_ref[...].astype(F32), jnp.zeros((128, PAD - ROPE), F32)], 1)
    xbuf[...] = jnp.zeros_like(xbuf)
    for t in range(2):
        for q in range(2):
            for hf in range(2):
                for jb in range(3):
                    src = 0 if jb == 0 else hf * 2 + jb
                    xbuf[pl.ds(hf * 512 + (t * 2 + q) * 3 + jb, 32, stride=16), :] = keyf[
                        src, pl.ds(t * GROUP + q, 32, stride=2), :
                    ]
    send1[...] = xbuf[...].astype(BF16).reshape(64, 16, 128)
    recvb[...] = jnp.zeros_like(recvb)

    sub = lax.broadcasted_iota(jnp.int32, (8, 128), 0)
    row = jnp.broadcast_to(order_row[...], (8, 128))
    zero8 = jnp.zeros((8, 128), F32)

    def fill(n, carry):
        which = lax.div(n, 32)
        o = lax.rem(n, 32)
        group = order_sm[2 * (2 * o + parity) + which]
        hot = jnp.where(row == sub + (group - (SPAN - 1)), 1.0, 0.0).astype(F32)
        upper = jnp.concatenate([hot, zero8], 1)
        lower = jnp.concatenate([zero8, hot], 1)
        onehot[pl.ds(pl.multiple_of(n * 16, 16), 16), :] = jnp.concatenate([upper, lower], 0).astype(BF16)
        return carry

    lax.fori_loop(0, 64, fill, 0)

    @pl.when(core == 0)
    def _():
        pl.semaphore_wait(barrier, 33)

    @pl.when(core == 1)
    def _():
        pl.semaphore_wait(barrier, 34)

    def send_piece(src, dst_buf, sem_s, sem_r, o):
        pltpu.make_async_remote_copy(
            src_ref=src, dst_ref=dst_buf.at[seq_par, place], send_sem=sem_s, recv_sem=sem_r,
            device_id=peer(o), device_id_type=MESH,
        ).start()

    def phase1(i, carry):
        o = lax.rem(place + i, 32)
        send_piece(send1.at[2 * o + parity], recv1, s1, r1, o)
        return carry

    @pl.when(core == 0)
    def _():
        pltpu.make_async_copy(send1.at[seq], recv1.at[seq_par, place], r1).start()

    @pl.when(core == 1)
    def _():
        send_piece(send1.at[2 * place + parity], recv1, s1x, r1, place)

    lax.fori_loop(1, 32, phase1, 0)
    pltpu.make_async_copy(recv1.at[parity], recv1.at[parity], r1).wait()
    cross1 = pltpu.make_async_remote_copy(
        src_ref=recv1.at[parity], dst_ref=recv1.at[parity], send_sem=s1c, recv_sem=r1c,
        device_id=twin, device_id_type=MESH,
    )
    cross1.start()
    pltpu.make_async_copy(recv1.at[other], recv1.at[other], r1c).wait()

    xbuf[...] = recv1[...].reshape(1024, 128).astype(F32)
    for q in range(2):
        for t in range(2):
            for jb in range(3):
                gather2[(q * 2 + t) * 64:(q * 2 + t + 1) * 64, jb * 128:(jb + 1) * 128] = xbuf[
                    pl.ds((t * 2 + q) * 3 + jb, 64, stride=16), :
                ].astype(BF16)

    def send_window(which, o, sem_s):
        @pl.when(half == 0)
        def _():
            pltpu.make_async_remote_copy(
                src_ref=send2.at[which, o], dst_ref=window.at[which, pair, seq_par, :, pl.ds(0, 384)],
                send_sem=sem_s, recv_sem=r2.at[which], device_id=peer(o), device_id_type=MESH,
            ).start()

        @pl.when(half == 1)
        def _():
            pltpu.make_async_remote_copy(
                src_ref=send2.at[which, o, :, pl.ds(128, 256)],
                dst_ref=window.at[which, pair, seq_par, :, pl.ds(384, 256)],
                send_sem=sem_s, recv_sem=r2.at[which], device_id=peer(o), device_id_type=MESH,
            ).start()

    for which in range(2):
        picked = dot_nn(onehot[which * 512:(which + 1) * 512, :], gather2[...])
        send2[which] = picked.astype(BF16).reshape(32, 16, 384)

        @pl.when(core == 0)
        def _():
            @pl.when(half == 0)
            def _():
                pltpu.make_async_copy(
                    send2.at[which, place], window.at[which, pair, seq_par, :, pl.ds(0, 384)], r2.at[which]
                ).start()

            @pl.when(half == 1)
            def _():
                pltpu.make_async_copy(
                    send2.at[which, place, :, pl.ds(128, 256)],
                    window.at[which, pair, seq_par, :, pl.ds(384, 256)], r2.at[which],
                ).start()

        @pl.when(core == 1)
        def _():
            send_window(which, place, s2x.at[which])

        def phase2(i, carry):
            send_window(which, lax.rem(place + i, 32), s2.at[which])
            return carry

        lax.fori_loop(1, 32, phase2, 0)

    for load in loads:
        load.wait()

    def project(h, carry):
        cols = pl.ds(pl.multiple_of(h * NOPE, NOPE), NOPE)
        rows = pl.ds(pl.multiple_of(h * GROUP, GROUP), GROUP)
        ql = dot_nt(qn[:, cols], uk[:, cols]).astype(BF16)
        gl = dot_nt(gout[:, cols], uv[:, cols]).astype(BF16)
        for w in range(2):
            qfull[w, rows, pl.ds(PAD, LATENT)] = ql[w * GROUP:(w + 1) * GROUP]
            glow[w, rows, :] = gl[w * GROUP:(w + 1) * GROUP]
        return carry

    lax.fori_loop(0, HEAD_DEV, project, 0)

    def rotary(m, carry):
        two = qr[:, pl.ds(pl.multiple_of(m * 128, 128), 128)].astype(F32)
        even = jnp.where(lanes < ROPE, two, 0.0).astype(BF16)
        odd = jnp.where(lanes < ROPE, pltpu.roll(two, ROPE, 1), 0.0).astype(BF16)
        for w in range(2):
            qfull[w, pl.ds(pl.multiple_of(m * 128, 128), GROUP), pl.ds(0, PAD)] = even[w * GROUP:(w + 1) * GROUP]
            qfull[w, pl.ds(pl.multiple_of(m * 128 + GROUP, GROUP), GROUP), pl.ds(0, PAD)] = odd[
                w * GROUP:(w + 1) * GROUP
            ]
        return carry

    lax.fori_loop(0, HEAD_DEV // 2, rotary, 0)

    col = lax.broadcasted_iota(jnp.int32, (GROUP, KEYS), 1)
    slot = lax.rem(col, SPAN)
    key_row = lax.div(col, SPAN)
    query_row = lax.broadcasted_iota(jnp.int32, (GROUP, KEYS), 0)
    for which in range(2):
        group = order_sm[2 * seq + which]
        seen = jnp.sum(mask_ref[pl.ds(group, 1), :], axis=1, keepdims=True)
        allowed = (slot >= SPAN - seen) & ((slot < SPAN - 1) | (key_row <= query_row))
        bias[which] = jnp.where(allowed, 0.0, -1e30).astype(F32)

    def send_grad(which, o, sem_s):
        dst = lax.div(o, 2)
        hf = lax.div(o, 16)

        @pl.when(hf == 0)
        def _():
            pltpu.make_async_remote_copy(
                src_ref=dmine.at[which, lax.rem(o, 16), :, pl.ds(0, 384)], dst_ref=recvb.at[which, place],
                send_sem=sem_s, recv_sem=r4.at[which], device_id=peer(o), device_id_type=MESH,
            ).start()

        @pl.when(hf == 1)
        def _():
            pltpu.make_async_remote_copy(
                src_ref=dmine.at[which, lax.rem(o, 16), :, pl.ds(384, 256)],
                dst_ref=recvb.at[which, place, :, pl.ds(128, 256)],
                send_sem=sem_s, recv_sem=r4.at[which], device_id=peer(o), device_id_type=MESH,
            ).start()

    cross2 = []
    for which in range(2):
        pltpu.make_async_copy(window.at[which, :, parity], window.at[which, :, parity], r2.at[which]).wait()
        cross2.append(pltpu.make_async_remote_copy(
            src_ref=window.at[which, :, parity], dst_ref=window.at[which, :, parity],
            send_sem=s2c.at[which], recv_sem=r2c.at[which], device_id=twin, device_id_type=MESH,
        ))
        cross2[which].start()
        pltpu.make_async_copy(window.at[which, :, other], window.at[which, :, other], r2c.at[which]).wait()

        def attend(n, carry):
            rows = pl.ds(pl.multiple_of(n * BLOCK, BLOCK), BLOCK)
            keys = window[which].reshape(KEYS, WIDTH)
            lat = keys[:, PAD:]
            scores = dot_nt(qfull[which, rows, :], keys) * SCALE2
            scores = (scores.reshape(BLOCK // GROUP, GROUP, KEYS) + bias[which][None]).reshape(BLOCK, KEYS)
            top = jnp.max(scores, axis=1, keepdims=True)
            weights = jnp.exp2(scores - top)
            normed = weights * (1.0 / jnp.sum(weights, axis=1, keepdims=True))
            low = normed.astype(BF16)
            grad_prob = dot_nt(glow[which, rows, :], lat)
            prod = normed * grad_prob
            delta = jnp.sum(prod, axis=1, keepdims=True)
            ds = (prod - normed * delta).astype(BF16)
            probs[rows, :] = low
            dscore[rows, :] = ds
            ol = dot_nn(low, lat).astype(BF16)
            gq = (dot_nn(ds, keys) * SCALE).astype(BF16)
            for j in range(BLOCK // GROUP):
                piece = slice(j * GROUP, (j + 1) * GROUP)
                olat[n * (BLOCK // GROUP) + j, which * GROUP:(which + 1) * GROUP, :] = ol[piece]
                gqlat[n * (BLOCK // GROUP) + j, which * GROUP:(which + 1) * GROUP, :] = gq[piece, PAD:]
            for j in range(0, BLOCK // GROUP, 2):
                two = jnp.concatenate(
                    [gq[j * GROUP:(j + 1) * GROUP, :ROPE], gq[(j + 1) * GROUP:(j + 2) * GROUP, :ROPE]], 1
                )
                gqr_v[
                    which * GROUP:(which + 1) * GROUP,
                    pl.ds(pl.multiple_of(n * (BLOCK // 2 * 2) + j * ROPE, 128), 128),
                ] = two
            return carry

        lax.fori_loop(0, ROWS // BLOCK, attend, 0)

        def key_grad(n, carry):
            krows = pl.ds(pl.multiple_of(n * 256, 256), 256)
            first = dot_tn(dscore[:, krows], qfull[which]) * SCALE
            second = dot_tn(probs[:, krows], glow[which])
            total = jnp.concatenate([first[:, :PAD], first[:, PAD:] + second], 1)
            dwin[which, pl.ds(n * 8, 8)] = total.reshape(8, 2, 16, WIDTH)
            return carry

        lax.fori_loop(0, KEYS // 256, key_grad, 0)

        dsend[which] = dwin[which, :, other].astype(BF16)
        cross3 = pltpu.make_async_remote_copy(
            src_ref=dsend.at[which], dst_ref=dpair.at[which], send_sem=s3c.at[which], recv_sem=r3c.at[which],
            device_id=twin, device_id_type=MESH,
        )
        cross3.start()
        cross3.wait_recv()
        dmine[which] = (dwin[which, :, parity] + dpair[which].astype(F32)).astype(BF16)

        @pl.when(core == 0)
        def _():
            @pl.when(half == 0)
            def _():
                pltpu.make_async_copy(
                    dmine.at[which, lax.rem(place, 16), :, pl.ds(0, 384)], recvb.at[which, place], r4.at[which]
                ).start()

            @pl.when(half == 1)
            def _():
                pltpu.make_async_copy(
                    dmine.at[which, lax.rem(place, 16), :, pl.ds(384, 256)],
                    recvb.at[which, place, :, pl.ds(128, 256)], r4.at[which],
                ).start()

        @pl.when(core == 1)
        def _():
            send_grad(which, place, s4x.at[which])

        def phase4(i, carry):
            send_grad(which, lax.rem(place + i, 32), s4.at[which])
            return carry

        lax.fori_loop(1, 32, phase4, 0)

    def unproject(h, carry):
        cols = pl.ds(pl.multiple_of(h * NOPE, NOPE), NOPE)
        out_v[:, cols] = dot_nn(olat[h], uv[:, cols]).astype(BF16)
        gqn_v[:, cols] = dot_nn(gqlat[h], uk[:, cols]).astype(BF16)
        return carry

    lax.fori_loop(0, HEAD_DEV, unproject, 0)
    stores = [
        pltpu.make_async_copy(src, dst, outsem.at[n])
        for n, (src, dst) in enumerate([(out_v, out_hbm), (gqn_v, gqn_hbm), (gqr_v, gqr_hbm)])
    ]
    for store in stores:
        store.start()

    total = jnp.zeros((256, 384), F32)
    for which in range(2):
        @pl.when(half == 0)
        def _():
            pltpu.make_async_copy(recvb.at[which], recvb.at[which], r4.at[which]).wait()

        @pl.when(half == 1)
        def _():
            ref = recvb.at[which, :, :, pl.ds(128, 256)]
            pltpu.make_async_copy(ref, ref, r4.at[which]).wait()

        total = total + dot_tn(onehot[which * 512:(which + 1) * 512, :], recvb[which].reshape(512, 384))
    asum[...] = total.reshape(4, 2, 32, 384)
    cross5 = pltpu.make_async_remote_copy(
        src_ref=asum.at[:, other], dst_ref=apair, send_sem=s5, recv_sem=r5, device_id=twin, device_id_type=MESH,
    )
    cross5.start()
    cross5.wait_recv()
    bsum[...] = asum[:, parity] + apair[...]
    cross6 = pltpu.make_async_remote_copy(
        src_ref=bsum, dst_ref=bpair, send_sem=s6, recv_sem=r6, device_id=far, device_id_type=MESH,
    )
    cross6.start()
    cross6.wait_recv()

    for q in range(2):
        for t in range(2):
            final = bsum[q * 2 + t] + bpair[q * 2 + t]
            for jb in range(3):
                xbuf[pl.ds((t * 2 + q) * 3 + jb, 32, stride=16), :] = final[:, jb * 128:(jb + 1) * 128]
    send4[...] = xbuf[pl.ds(0, 512), :].astype(BF16).reshape(32, 16, 128)

    @pl.when(core == 0)
    def _():
        pltpu.make_async_copy(send4.at[place], recv4.at[seq_par, place], r7).start()

    @pl.when(core == 1)
    def _():
        send_piece(send4.at[place], recv4, s7x, r7, place)

    def phase7(i, carry):
        o = lax.rem(place + i, 32)
        send_piece(send4.at[o], recv4, s7, r7, o)
        return carry

    lax.fori_loop(1, 32, phase7, 0)
    pltpu.make_async_copy(recv4.at[parity], recv4.at[parity], r7).wait()
    cross7 = pltpu.make_async_remote_copy(
        src_ref=recv4.at[parity], dst_ref=recv4.at[parity], send_sem=s7c, recv_sem=r7c,
        device_id=twin, device_id_type=MESH,
    )
    cross7.start()
    pltpu.make_async_copy(recv4.at[other], recv4.at[other], r7c).wait()

    xbuf[...] = recv4[...].reshape(1024, 128).astype(F32)
    for t in range(2):
        for q in range(2):
            for pp in range(2):
                for hf in range(2):
                    for jb in range(3):
                        if jb == 0 and hf == 1:
                            continue
                        dst = 0 if jb == 0 else hf * 2 + jb
                        base = (pp * 32 + hf * 16) * 16 + (t * 2 + q) * 3 + jb
                        keyf[dst, pl.ds(t * GROUP + pp * 2 + q, 16, stride=4), :] = xbuf[
                            pl.ds(base, 16, stride=16), :
                        ]
    for b in range(4):
        glat_ref[:, b * 128:(b + 1) * 128] = keyf[b + 1].astype(BF16)
    grope_ref[...] = keyf[0][:, :ROPE].astype(BF16)

    def drain(ref, sem):
        pltpu.make_async_copy(ref, ref, sem).wait()

    drain(send1.at[pl.ds(0, 31)], s1)
    drain(send4.at[pl.ds(0, 31)], s7)
    cross1.wait_send()
    cross5.wait_send()
    cross6.wait_send()
    cross7.wait_send()

    @pl.when(core == 1)
    def _():
        drain(send1.at[0], s1x)
        drain(send4.at[0], s7x)

    for which in range(2):
        cross2[which].wait_send()
        drain(dsend.at[which], s3c.at[which])

        @pl.when(half == 0)
        def _():
            drain(send2.at[which, pl.ds(0, 31)], s2.at[which])

            @pl.when(core == 1)
            def _():
                drain(send2.at[which, 0], s2x.at[which])
                drain(recvb.at[which, 0], s4x.at[which])

        @pl.when(half == 1)
        def _():
            drain(send2.at[which, pl.ds(0, 31), :, pl.ds(128, 256)], s2.at[which])

            @pl.when(core == 1)
            def _():
                drain(send2.at[which, 0, :, pl.ds(128, 256)], s2x.at[which])
                drain(recvb.at[which, 0, :, pl.ds(128, 256)], s4x.at[which])

        @pl.when(half == 0)
        def _():
            drain(recvb.at[which, pl.ds(0, 15)], s4.at[which])
            drain(recvb.at[which, pl.ds(0, 16), :, pl.ds(128, 256)], s4.at[which])

        @pl.when(half == 1)
        def _():
            drain(recvb.at[which, pl.ds(0, 16)], s4.at[which])
            drain(recvb.at[which, pl.ds(0, 15), :, pl.ds(128, 256)], s4.at[which])

    for store in stores:
        store.wait()


def local(
    query_nope, query_rope, latent, key_rope, up_key, up_value, grad_out, group_order, tile_mask
):
    order_row = group_order.reshape(32, 2, 2).transpose(2, 1, 0).reshape(1, 128)
    vmem = pl.BlockSpec(memory_space=pltpu.VMEM)
    smem = pl.BlockSpec(memory_space=pltpu.SMEM)
    hbm = pl.BlockSpec(memory_space=pl.ANY)
    dma = pltpu.SemaphoreType.DMA
    scratch = [
        pltpu.VMEM((128, 2048), BF16),
        pltpu.VMEM((128, 1024), BF16),
        pltpu.VMEM((LATENT, 2048), BF16),
        pltpu.VMEM((LATENT, 2048), BF16),
        pltpu.VMEM((128, 2048), BF16),
        pltpu.VMEM((128, 2048), BF16),
        pltpu.VMEM((128, 2048), BF16),
        pltpu.VMEM((128, 1024), BF16),
        pltpu.VMEM((5, 128, 128), F32),
        pltpu.VMEM((1024, 128), F32),
        pltpu.VMEM((64, 16, 128), BF16),
        pltpu.VMEM((2, 32, 16, 128), BF16),
        pltpu.VMEM((256, 384), BF16),
        pltpu.VMEM((1024, 256), BF16),
        pltpu.VMEM((2, 32, 16, 384), BF16),
        pltpu.VMEM((2, 16, 2, 16, WIDTH), BF16),
        pltpu.VMEM((2, ROWS, WIDTH), BF16),
        pltpu.VMEM((2, ROWS, LATENT), BF16),
        pltpu.VMEM((HEAD_DEV, 128, LATENT), BF16),
        pltpu.VMEM((HEAD_DEV, 128, LATENT), BF16),
        pltpu.VMEM((ROWS, KEYS), BF16),
        pltpu.VMEM((ROWS, KEYS), BF16),
        pltpu.VMEM((2, GROUP, KEYS), F32),
        pltpu.VMEM((2, 16, 2, 16, WIDTH), F32),
        pltpu.VMEM((2, 16, 16, WIDTH), BF16),
        pltpu.VMEM((2, 16, 16, WIDTH), BF16),
        pltpu.VMEM((2, 16, 16, WIDTH), BF16),
        pltpu.VMEM((2, 32, 16, 384), BF16),
        pltpu.VMEM((4, 2, 32, 384), F32),
        pltpu.VMEM((4, 32, 384), F32),
        pltpu.VMEM((4, 32, 384), F32),
        pltpu.VMEM((4, 32, 384), F32),
        pltpu.VMEM((32, 16, 128), BF16),
        pltpu.VMEM((2, 32, 16, 128), BF16),
        dma((5,)), dma((3,)),
        dma, dma, dma, dma, dma,
        dma((2,)), dma((2,)), dma((2,)), dma((2,)), dma((2,)),
        dma((2,)), dma((2,)),
        dma((2,)), dma((2,)), dma((2,)),
        dma, dma, dma, dma,
        dma, dma, dma, dma, dma,
    ]
    return pl.pallas_call(
        kernel,
        out_shape=(
            jax.ShapeDtypeStruct((128, 2048), BF16),
            jax.ShapeDtypeStruct((128, 2048), BF16),
            jax.ShapeDtypeStruct((128, 1024), BF16),
            jax.ShapeDtypeStruct((128, LATENT), BF16),
            jax.ShapeDtypeStruct((128, ROPE), BF16),
        ),
        in_specs=[hbm, hbm, vmem, vmem, hbm, hbm, hbm, smem, vmem, vmem],
        out_specs=(hbm, hbm, hbm, vmem, vmem),
        scratch_shapes=scratch,
        compiler_params=pltpu.CompilerParams(
            collective_id=0, has_side_effects=True, vmem_limit_bytes=56 << 20
        ),
    )(
        query_nope, query_rope, latent, key_rope, up_key, up_value, grad_out,
        group_order, order_row, tile_mask,
    )


def solution(mesh):
    placed = (
        P("seq", "head"),
        P("seq", "head"),
        P("seq", None),
        P("seq", None),
        P(None, "head"),
        P(None, "head"),
        P("seq", "head"),
        P(),
        P(),
    )
    return jax.shard_map(
        local,
        mesh=mesh,
        in_specs=placed,
        out_specs=(
            P("seq", "head"),
            P("seq", "head"),
            P("seq", "head"),
            P("seq", None),
            P("seq", None),
        ),
        check_vma=False,
    )
```

```python
import functools
import math

import jax
import jax.numpy as jnp
from jax import lax
from jax.experimental import pallas as pl
from jax.experimental.pallas import tpu as pltpu
from jax.sharding import PartitionSpec as P

HEAD_DEV = 16
LATENT = 512
ROPE = 64
NOPE = 128
SPAN = 8
GROUP = 64
PAD = 128
WIDTH = PAD + LATENT
KEYS = SPAN * GROUP
ROWS = HEAD_DEV * GROUP
MESH = pl.DeviceIdType.MESH
SCALE = (NOPE + ROPE) ** (-0.5)
SCALE2 = SCALE * math.log2(math.e)
BLOCK = 256
F32 = jnp.float32
BF16 = jnp.bfloat16


def dot_nt(a, b):
    return lax.dot_general(a, b, (((1,), (1,)), ((), ())), preferred_element_type=F32)


def dot_nn(a, b):
    return lax.dot_general(a, b, (((1,), (0,)), ((), ())), preferred_element_type=F32)


def dot_tn(a, b):
    return lax.dot_general(a, b, (((0,), (0,)), ((), ())), preferred_element_type=F32)


def kernel(
    qn_hbm, qr_hbm, lat_ref, rope_ref, uk_hbm, uv_hbm, go_hbm, order_sm, order_ref, mask_hbm,
    out_hbm, gqn_hbm, gqr_hbm, glat_ref, grope_ref,
    qn, qr, uk, uv, gout, mask_ref, out_v, gqn_v, gqr_v,
    keyf, xbuf, send1, recv1, gather2, onehot, send2, window,
    qfull, glow, olat, gqlat, probs, dscore, bias,
    dwin, dsend, dpair, dmine, recvb, send7, recv7, part, fpart, home,
    insem, outsem, s1, r1, s2, r2, s2c, r2c,
    s3c, r3c, s4, r4, s7, r7, s8, r8, s9, r9,
):
    seq = lax.axis_index("seq")
    head = lax.axis_index("head")
    core = lax.rem(head, 2)
    x = lax.div(seq, 16)
    z = lax.rem(lax.div(seq, 2), 8)
    y = lax.rem(seq, 2)
    plane = lax.div(z, 4)
    piece = x * 8 + lax.rem(z, 4) * 2 + y
    twin = (seq, head + 1 - 2 * core)
    far = (seq, lax.rem(head + 2, 4))

    def around(i):
        return lax.rem(seq + i, 64)

    def piece_of(device):
        return lax.div(device, 16) * 8 + lax.rem(lax.div(device, 2), 4) * 2 + lax.rem(device, 2)

    def near(o, sign):
        step = lax.div(o, 8)
        shift = step + 5 * lax.div(step, 2) - 6 * lax.div(step, 3) + 4 * core * lax.div(step, 3)
        xo = lax.rem(lax.div(o, 2), 4)
        nx = lax.rem(x + 4 + sign * xo, 4)
        nz = lax.rem(z + 8 + sign * shift, 8)
        ny = lax.rem(y + lax.rem(o, 2), 2)
        return nx * 16 + nz * 2 + ny

    loads = [
        pltpu.make_async_copy(src, dst, insem.at[n])
        for n, (src, dst) in enumerate(
            [(qn_hbm, qn), (qr_hbm, qr), (uk_hbm, uk), (uv_hbm, uv), (go_hbm, gout), (mask_hbm, mask_ref)]
        )
    ]
    for load in loads:
        load.start()

    barrier = pltpu.get_barrier_semaphore()

    def greet(i, carry):
        pl.semaphore_signal(barrier, inc=1, device_id=(around(i), head), device_id_type=MESH)
        return carry

    lax.fori_loop(1, 64, greet, 0)
    pl.semaphore_signal(barrier, inc=1, device_id=twin, device_id_type=MESH)
    pl.semaphore_signal(barrier, inc=1, device_id=far, device_id_type=MESH)

    lanes = lax.broadcasted_iota(jnp.int32, (128, PAD), 1)
    rope = jnp.concatenate([rope_ref[...].astype(F32), jnp.zeros((PAD - ROPE, 128), F32)], 0)
    keyf[0] = rope.T
    for b in range(2):
        keyf[b + 1] = lat_ref[:, pl.ds(pl.multiple_of(core * 256 + b * 128, 128), 128)].astype(F32)
    xbuf[...] = jnp.zeros_like(xbuf)
    for t in range(2):
        for q in range(2):
            for jb in range(3):
                xbuf[pl.ds((t * 2 + q) * 3 + jb, 32, stride=16), :] = keyf[
                    jb, pl.ds(t * GROUP + q, 32, stride=2), :
                ]
    send1[...] = xbuf[pl.ds(0, 512), :].astype(BF16).reshape(32, 16, 128)

    sub = lax.broadcasted_iota(jnp.int32, (8, 128), 0)
    cin = lax.broadcasted_iota(jnp.int32, (128, 128), 0)
    cout = lax.broadcasted_iota(jnp.int32, (128, 128), 1)
    reorder = jnp.where(cin == 2 * lax.rem(cout, 64) + lax.div(cout, 64), 1.0, 0.0).astype(BF16)
    plain = jnp.broadcast_to(order_ref[...].astype(F32).reshape(1, 128), (8, 128)).astype(BF16)
    row = dot_nn(plain, reorder)
    zero8 = jnp.zeros((8, 128), F32)

    def fill(n, carry):
        which = lax.div(n, 32)
        group = order_sm[2 * near(lax.rem(n, 32), 1) + which]
        hot = jnp.where(row == (sub + (group - (SPAN - 1))).astype(F32), 1.0, 0.0).astype(F32)
        upper = jnp.concatenate([hot, zero8], 1)
        lower = jnp.concatenate([zero8, hot], 1)
        onehot[pl.ds(pl.multiple_of(n * 16, 16), 16), :] = jnp.concatenate([upper, lower], 0).astype(BF16)
        return carry

    lax.fori_loop(0, 64, fill, 0)
    recvb[...] = jnp.zeros_like(recvb)
    pl.semaphore_wait(barrier, 65)

    pltpu.make_async_copy(send1.at[piece], recv1.at[seq], r1).start()

    def phase1(i, carry):
        dst = around(i)
        pltpu.make_async_remote_copy(
            src_ref=send1.at[piece_of(dst)], dst_ref=recv1.at[seq], send_sem=s1, recv_sem=r1,
            device_id=(dst, head), device_id_type=MESH,
        ).start()
        return carry

    lax.fori_loop(1, 64, phase1, 0)

    for load in loads:
        load.wait()

    def project(h, carry):
        cols = pl.ds(pl.multiple_of(h * NOPE, NOPE), NOPE)
        rows = pl.ds(pl.multiple_of(h * GROUP, GROUP), GROUP)
        ql = dot_nt(qn[:, cols], uk[:, cols]).astype(BF16)
        gl = dot_nt(gout[:, cols], uv[:, cols]).astype(BF16)
        for w in range(2):
            qfull[w, rows, pl.ds(PAD, LATENT)] = ql[w * GROUP:(w + 1) * GROUP]
            glow[w, rows, :] = gl[w * GROUP:(w + 1) * GROUP]
        return carry

    lax.fori_loop(0, HEAD_DEV, project, 0)

    pltpu.make_async_copy(recv1, recv1, r1).wait()
    xbuf[...] = recv1[...].reshape(1024, 128).astype(F32)
    for q in range(2):
        for t in range(2):
            for jb in range(3):
                gather2[(q * 2 + t) * 64:(q * 2 + t + 1) * 64, jb * 128:(jb + 1) * 128] = xbuf[
                    pl.ds((t * 2 + q) * 3 + jb, 64, stride=16), :
                ].astype(BF16)

    def half_of(ref, cr):
        return ref if cr == 0 else ref.at[:, pl.ds(128, 256)]

    def columns(cr):
        return pl.ds(0, 384) if cr == 0 else pl.ds(384, 256)

    def by_core(run):
        for cr in range(2):
            @pl.when(core == cr)
            def _():
                run(cr)

    for which in range(2):
        picked = dot_nn(onehot[which * 512:(which + 1) * 512, :], gather2[...])
        send2[which] = picked.astype(BF16).reshape(32, 16, 384)

        def send_windows(cr):
            pltpu.make_async_copy(
                half_of(send2.at[which, 0], cr), window.at[which, piece, :, columns(cr)], r2.at[which]
            ).start()

            def phase2(o, carry):
                pltpu.make_async_remote_copy(
                    src_ref=half_of(send2.at[which, o], cr), dst_ref=window.at[which, piece, :, columns(cr)],
                    send_sem=s2.at[which], recv_sem=r2.at[which],
                    device_id=(near(o, 1), head), device_id_type=MESH,
                ).start()
                return carry

            lax.fori_loop(1, 32, phase2, 0)

        by_core(send_windows)

    def rotary(m, carry):
        two = qr[:, pl.ds(pl.multiple_of(m * 128, 128), 128)].astype(F32)
        even = jnp.where(lanes < ROPE, two, 0.0).astype(BF16)
        odd = jnp.where(lanes < ROPE, pltpu.roll(two, ROPE, 1), 0.0).astype(BF16)
        for w in range(2):
            qfull[w, pl.ds(pl.multiple_of(m * 128, 128), GROUP), pl.ds(0, PAD)] = even[w * GROUP:(w + 1) * GROUP]
            qfull[w, pl.ds(pl.multiple_of(m * 128 + GROUP, GROUP), GROUP), pl.ds(0, PAD)] = odd[
                w * GROUP:(w + 1) * GROUP
            ]
        return carry

    lax.fori_loop(0, HEAD_DEV // 2, rotary, 0)

    col = lax.broadcasted_iota(jnp.int32, (GROUP, KEYS), 1)
    slot = lax.rem(col, SPAN)
    key_row = lax.div(col, SPAN)
    query_row = lax.broadcasted_iota(jnp.int32, (GROUP, KEYS), 0)
    for which in range(2):
        group = order_sm[2 * seq + which]
        seen = jnp.sum(mask_ref[pl.ds(group, 1), :], axis=1, keepdims=True)
        allowed = (slot >= SPAN - seen) & ((slot < SPAN - 1) | (key_row <= query_row))
        bias[which] = jnp.where(allowed, 0.0, -1e30).astype(F32)

    def cross_copy(src, dst, sem_s, sem_r):
        return pltpu.make_async_remote_copy(
            src_ref=src, dst_ref=dst, send_sem=sem_s, recv_sem=sem_r, device_id=twin, device_id_type=MESH
        )

    def share_window(which):
        def run(cr):
            ref = window.at[which, :, :, columns(cr)]
            pltpu.make_async_copy(ref, ref, r2.at[which]).wait()
            cross_copy(ref, ref, s2c.at[which], r2c.at[which]).start()

        by_core(run)

    def await_window(which):
        def run(cr):
            ref = window.at[which, :, :, columns(1 - cr)]
            pltpu.make_async_copy(ref, ref, r2c.at[which]).wait()

        by_core(run)

    def attend_from(which, first, last):
        def attend(n, carry):
            rows = pl.ds(pl.multiple_of(n * BLOCK, BLOCK), BLOCK)
            keys = window[which].reshape(KEYS, WIDTH)
            lat = keys[:, PAD:]
            scores = dot_nt(qfull[which, rows, :], keys) * SCALE2
            scores = (scores.reshape(BLOCK // GROUP, GROUP, KEYS) + bias[which][None]).reshape(BLOCK, KEYS)
            top = jnp.max(scores, axis=1, keepdims=True)
            weights = jnp.exp2(scores - top)
            normed = weights * (1.0 / jnp.sum(weights, axis=1, keepdims=True))
            low = normed.astype(BF16)
            grad_prob = dot_nt(glow[which, rows, :], lat)
            prod = normed * grad_prob
            delta = jnp.sum(prod, axis=1, keepdims=True)
            ds = (prod - normed * delta).astype(BF16)
            probs[rows, :] = low
            dscore[rows, :] = ds
            ol = dot_nn(low, lat).astype(BF16)
            gq = (dot_nn(ds, keys) * SCALE).astype(BF16)
            for j in range(BLOCK // GROUP):
                part_rows = slice(j * GROUP, (j + 1) * GROUP)
                olat[n * (BLOCK // GROUP) + j, which * GROUP:(which + 1) * GROUP, :] = ol[part_rows]
                gqlat[n * (BLOCK // GROUP) + j, which * GROUP:(which + 1) * GROUP, :] = gq[part_rows, PAD:]
            for j in range(0, BLOCK // GROUP, 2):
                two = jnp.concatenate(
                    [gq[j * GROUP:(j + 1) * GROUP, :ROPE], gq[(j + 1) * GROUP:(j + 2) * GROUP, :ROPE]], 1
                )
                gqr_v[
                    which * GROUP:(which + 1) * GROUP, pl.ds(pl.multiple_of(n * BLOCK + j * ROPE, 128), 128)
                ] = two
            return carry

        lax.fori_loop(first, last, attend, 0)

    def key_grads(which):
        def key_grad(n, carry):
            krows = pl.ds(pl.multiple_of(n * 256, 256), 256)
            first = dot_tn(dscore[:, krows], qfull[which]) * SCALE
            second = dot_tn(probs[:, krows], glow[which])
            total = jnp.concatenate([first[:, :PAD], first[:, PAD:] + second], 1)
            dwin[which, pl.ds(n * 16, 16)] = total.reshape(16, 16, WIDTH)
            return carry

        lax.fori_loop(0, KEYS // 256, key_grad, 0)

    def share_grads(which):
        def run(cr):
            rest = columns(1 - cr)
            into = pl.ds(128, 256) if cr == 0 else pl.ds(0, 384)
            dsend[which, :, :, into] = dwin[which, :, :, rest].astype(BF16)
            cross_copy(
                dsend.at[which, :, :, into], dpair.at[which, :, :, into], s3c.at[which], r3c.at[which]
            ).start()

        by_core(run)

    def send_grads(which):
        def run(cr):
            into = pl.ds(0, 384) if cr == 0 else pl.ds(128, 256)
            ref = dpair.at[which, :, :, into]
            pltpu.make_async_copy(ref, ref, r3c.at[which]).wait()
            dmine[which, :, :, into] = (
                dwin[which, :, :, columns(cr)] + dpair[which, :, :, into].astype(F32)
            ).astype(BF16)
            pltpu.make_async_copy(
                half_of(dmine.at[which, piece], cr), half_of(recvb.at[which, 0], cr), r4.at[which]
            ).start()

            def phase4(o, carry):
                dst = near(o, -1)
                pltpu.make_async_remote_copy(
                    src_ref=half_of(dmine.at[which, piece_of(dst)], cr), dst_ref=half_of(recvb.at[which, o], cr),
                    send_sem=s4.at[which], recv_sem=r4.at[which], device_id=(dst, head), device_id_type=MESH,
                ).start()
                return carry

            lax.fori_loop(1, 32, phase4, 0)

        by_core(run)

    blocks = ROWS // BLOCK
    share_window(0)
    await_window(0)
    attend_from(0, 0, blocks)
    share_window(1)
    key_grads(0)
    share_grads(0)
    await_window(1)
    attend_from(1, 0, 1)
    send_grads(0)
    attend_from(1, 1, blocks)
    key_grads(1)
    share_grads(1)
    send_grads(1)

    def unproject(h, carry):
        cols = pl.ds(pl.multiple_of(h * NOPE, NOPE), NOPE)
        out_v[:, cols] = dot_nn(olat[h], uv[:, cols]).astype(BF16)
        gqn_v[:, cols] = dot_nn(gqlat[h], uk[:, cols]).astype(BF16)
        return carry

    lax.fori_loop(0, HEAD_DEV, unproject, 0)
    stores = [
        pltpu.make_async_copy(src, dst, outsem.at[n])
        for n, (src, dst) in enumerate([(out_v, out_hbm), (gqn_v, gqn_hbm), (gqr_v, gqr_hbm)])
    ]
    for store in stores:
        store.start()

    total = jnp.zeros((256, 384), F32)
    for which in range(2):
        def await_grads(cr):
            ref = recvb.at[which] if cr == 0 else recvb.at[which, :, :, pl.ds(128, 256)]
            pltpu.make_async_copy(ref, ref, r4.at[which]).wait()

        by_core(await_grads)
        total = total + dot_tn(onehot[which * 512:(which + 1) * 512, :], recvb[which].reshape(512, 384))
    for q in range(2):
        for t in range(2):
            for jb in range(3):
                xbuf[pl.ds((t * 2 + q) * 3 + jb, 64, stride=16), :] = total[
                    (q * 2 + t) * 64:(q * 2 + t + 1) * 64, jb * 128:(jb + 1) * 128
                ]
    send7[...] = xbuf[...].astype(BF16).reshape(64, 16, 128)

    pltpu.make_async_copy(send7.at[seq], recv7.at[plane, piece], r7).start()

    def phase7(i, carry):
        dst = around(i)
        pltpu.make_async_remote_copy(
            src_ref=send7.at[dst], dst_ref=recv7.at[plane, piece], send_sem=s7, recv_sem=r7,
            device_id=(dst, head), device_id_type=MESH,
        ).start()
        return carry

    lax.fori_loop(1, 64, phase7, 0)
    pltpu.make_async_copy(recv7, recv7, r7).wait()
    xbuf[pl.ds(0, 512), :] = (recv7[0].astype(F32) + recv7[1].astype(F32)).reshape(512, 128)
    for t in range(2):
        for q in range(2):
            for jb in range(3):
                keyf[jb, pl.ds(t * GROUP + q, 32, stride=2), :] = xbuf[
                    pl.ds((t * 2 + q) * 3 + jb, 32, stride=16), :
                ]
    part[...] = keyf[...].astype(BF16)

    def add_far(cr):
        blocks3 = pl.ds(0, 3) if cr == 0 else pl.ds(1, 2)
        mine = pl.ds(0, 3) if cr == 0 else pl.ds(3, 2)
        rest = pl.ds(3, 2) if cr == 0 else pl.ds(0, 3)
        copy = pltpu.make_async_remote_copy(
            src_ref=part.at[blocks3], dst_ref=fpart.at[blocks3], send_sem=s8, recv_sem=r8,
            device_id=far, device_id_type=MESH,
        )
        copy.start()
        copy.wait_recv()
        home[mine] = (part[blocks3].astype(F32) + fpart[blocks3].astype(F32)).astype(BF16)
        cross_copy(home.at[mine], home.at[mine], s9, r9).start()
        pltpu.make_async_copy(home.at[rest], home.at[rest], r9).wait()
        copy.wait_send()
        pltpu.make_async_copy(home.at[mine], home.at[mine], s9).wait()

    by_core(add_far)
    for b in range(4):
        glat_ref[:, b * 128:(b + 1) * 128] = home[b + 1]
    grope_ref[...] = home[0].astype(F32).T[:ROPE].astype(BF16)

    def drain(ref, sem):
        pltpu.make_async_copy(ref, ref, sem).wait()

    drain(recv1.at[pl.ds(0, 63)], s1)
    drain(send7.at[pl.ds(0, 63)], s7)

    def drain_halves(cr):
        for which in range(2):
            own = pl.ds(0, 384) if cr == 0 else pl.ds(128, 256)
            rest = pl.ds(128, 256) if cr == 0 else pl.ds(0, 384)
            drain(send2.at[which, pl.ds(0, 31), :, own], s2.at[which])
            drain(dmine.at[which, pl.ds(0, 31), :, own], s4.at[which])
            drain(window.at[which, :, :, columns(cr)], s2c.at[which])
            drain(dsend.at[which, :, :, rest], s3c.at[which])

    by_core(drain_halves)
    for store in stores:
        store.wait()


def copy_kernel(*refs):
    count = (len(refs) - 2) // 3
    srcs, dsts, held = refs[:count], refs[count:2 * count], refs[2 * count:3 * count]
    insem, outsem = refs[3 * count:]
    reads = [pltpu.make_async_copy(srcs[n], held[n], insem.at[n]) for n in range(count)]
    writes = [pltpu.make_async_copy(held[n], dsts[n], outsem.at[n]) for n in range(count)]
    for read in reads:
        read.start()
    for read, write in zip(reads, writes):
        read.wait()
        write.start()
    for write in writes:
        write.wait()


def local(
    query_nope, query_rope, latent, key_rope, up_key, up_value, grad_out, group_order, tile_mask
):
    vmem = pl.BlockSpec(memory_space=pltpu.VMEM)
    smem = pl.BlockSpec(memory_space=pltpu.SMEM)
    hbm = pl.BlockSpec(memory_space=pl.ANY)
    dma = pltpu.SemaphoreType.DMA
    scratch = [
        pltpu.VMEM((128, 2048), BF16),
        pltpu.VMEM((128, 1024), BF16),
        pltpu.VMEM((LATENT, 2048), BF16),
        pltpu.VMEM((LATENT, 2048), BF16),
        pltpu.VMEM((128, 2048), BF16),
        pltpu.VMEM((128, 128), jnp.int32),
        pltpu.VMEM((128, 2048), BF16),
        pltpu.VMEM((128, 2048), BF16),
        pltpu.VMEM((128, 1024), BF16),
        pltpu.VMEM((3, 128, 128), F32),
        pltpu.VMEM((1024, 128), F32),
        pltpu.VMEM((32, 16, 128), BF16),
        pltpu.VMEM((64, 16, 128), BF16),
        pltpu.VMEM((256, 384), BF16),
        pltpu.VMEM((1024, 256), BF16),
        pltpu.VMEM((2, 32, 16, 384), BF16),
        pltpu.VMEM((2, 32, 16, WIDTH), BF16),
        pltpu.VMEM((2, ROWS, WIDTH), BF16),
        pltpu.VMEM((2, ROWS, LATENT), BF16),
        pltpu.VMEM((HEAD_DEV, 128, LATENT), BF16),
        pltpu.VMEM((HEAD_DEV, 128, LATENT), BF16),
        pltpu.VMEM((ROWS, KEYS), BF16),
        pltpu.VMEM((ROWS, KEYS), BF16),
        pltpu.VMEM((2, GROUP, KEYS), F32),
        pltpu.VMEM((2, 32, 16, WIDTH), F32),
        pltpu.VMEM((2, 32, 16, 384), BF16),
        pltpu.VMEM((2, 32, 16, 384), BF16),
        pltpu.VMEM((2, 32, 16, 384), BF16),
        pltpu.VMEM((2, 32, 16, 384), BF16),
        pltpu.VMEM((64, 16, 128), BF16),
        pltpu.VMEM((2, 32, 16, 128), BF16),
        pltpu.VMEM((3, 128, 128), BF16),
        pltpu.VMEM((3, 128, 128), BF16),
        pltpu.VMEM((5, 128, 128), BF16),
        dma((6,)), dma((3,)),
        dma, dma,
        dma((2,)), dma((2,)), dma((2,)), dma((2,)),
        dma((2,)), dma((2,)),
        dma((2,)), dma((2,)),
        dma, dma, dma, dma, dma, dma,
    ]
    shapes = (
        jax.ShapeDtypeStruct((128, 2048), BF16),
        jax.ShapeDtypeStruct((128, 2048), BF16),
        jax.ShapeDtypeStruct((128, 1024), BF16),
        jax.ShapeDtypeStruct((128, LATENT), BF16),
        jax.ShapeDtypeStruct((ROPE, 128), BF16),
    )
    results = pl.pallas_call(
        kernel,
        out_shape=shapes,
        in_specs=[hbm, hbm, vmem, vmem, hbm, hbm, hbm, smem, vmem, hbm],
        out_specs=(hbm, hbm, hbm, vmem, vmem),
        scratch_shapes=scratch,
        compiler_params=pltpu.CompilerParams(
            collective_id=0, has_side_effects=True, vmem_limit_bytes=56 << 20
        ),
    )(
        query_nope, query_rope, latent, key_rope.T, up_key, up_value, grad_out,
        group_order, group_order, tile_mask,
    )
    out, gqn, gqr, glat, grope = pl.pallas_call(
        copy_kernel,
        out_shape=shapes,
        in_specs=[hbm] * 5,
        out_specs=(hbm,) * 5,
        scratch_shapes=[pltpu.VMEM(a.shape, a.dtype) for a in shapes] + [dma((5,)), dma((5,))],
    )(*results)
    return out, gqn, gqr, glat, grope.T


def solution(mesh):
    placed = (
        P("seq", "head"),
        P("seq", "head"),
        P("seq", None),
        P("seq", None),
        P(None, "head"),
        P(None, "head"),
        P("seq", "head"),
        P(),
        P(),
    )
    return jax.shard_map(
        local,
        mesh=mesh,
        in_specs=placed,
        out_specs=(
            P("seq", "head"),
            P("seq", "head"),
            P("seq", "head"),
            P("seq", None),
            P("seq", None),
        ),
        check_vma=False,
    )
```

```python
import functools
import math

import jax
import jax.numpy as jnp
from jax import lax
from jax.experimental import pallas as pl
from jax.experimental.pallas import tpu as pltpu
from jax.sharding import PartitionSpec as P

HEAD_DEV = 16
LATENT = 512
ROPE = 64
NOPE = 128
SPAN = 8
GROUP = 64
PAD = 128
WIDTH = PAD + LATENT
KEYS = SPAN * GROUP
ROWS = HEAD_DEV * GROUP
MESH = pl.DeviceIdType.MESH
SCALE = (NOPE + ROPE) ** (-0.5)
SCALE2 = SCALE * math.log2(math.e)
BLOCK = 512
SUB = 256
F32 = jnp.float32
BF16 = jnp.bfloat16


def dot_nt(a, b):
    return lax.dot_general(a, b, (((1,), (1,)), ((), ())), preferred_element_type=F32)


def dot_nn(a, b):
    return lax.dot_general(a, b, (((1,), (0,)), ((), ())), preferred_element_type=F32)


def dot_tn(a, b):
    return lax.dot_general(a, b, (((0,), (0,)), ((), ())), preferred_element_type=F32)


def kernel(
    qn_hbm, qr_hbm, lat_ref, rope_ref, uk_hbm, uv_hbm, go_hbm, order_sm, order_ref, mask_hbm,
    out_hbm, gqn_hbm, gqr_hbm, glat_ref, grope_ref,
    qn, qr, uk, uv, gout, mask_ref, out_v, gqn_v, gqr_v,
    keyf, xbuf, send1, recv1, gather2, onehot, send2, window,
    qfull, glow, olat, gqlat, probs, dscore, bias,
    dwin, dsend, dpair, dmine, recvb, onehot_t, send7, recv7, part, fpart, home,
    insem, outsem, s1, r1, s2, r2, s2c, r2c,
    s3c, r3c, s4, r4, s7, r7, s8, r8, s9, r9,
):
    seq = lax.axis_index("seq")
    head = lax.axis_index("head")
    core = lax.rem(head, 2)
    x = lax.div(seq, 16)
    z = lax.rem(lax.div(seq, 2), 8)
    y = lax.rem(seq, 2)
    plane = lax.div(z, 4)
    piece = x * 8 + lax.rem(z, 4) * 2 + y
    twin = (seq, head + 1 - 2 * core)
    far = (seq, lax.rem(head + 2, 4))

    def around(i):
        return lax.rem(seq + i, 64)

    def piece_of(device):
        return lax.div(device, 16) * 8 + lax.rem(lax.div(device, 2), 4) * 2 + lax.rem(device, 2)

    def near(o, sign):
        step = lax.div(o, 8)
        shift = step + 5 * lax.div(step, 2) - 6 * lax.div(step, 3) + 4 * core * lax.div(step, 3)
        xo = lax.rem(lax.div(o, 2), 4)
        nx = lax.rem(x + 4 + sign * xo, 4)
        nz = lax.rem(z + 8 + sign * shift, 8)
        ny = lax.rem(y + lax.rem(o, 2), 2)
        return nx * 16 + nz * 2 + ny

    loads = [
        pltpu.make_async_copy(src, dst, insem.at[n])
        for n, (src, dst) in enumerate(
            [(qn_hbm, qn), (qr_hbm, qr), (uk_hbm, uk), (uv_hbm, uv), (go_hbm, gout), (mask_hbm, mask_ref)]
        )
    ]
    for load in loads:
        load.start()

    barrier = pltpu.get_barrier_semaphore()

    def greet(i, carry):
        pl.semaphore_signal(barrier, inc=1, device_id=(around(i), head), device_id_type=MESH)
        return carry

    lax.fori_loop(1, 64, greet, 0)
    pl.semaphore_signal(barrier, inc=1, device_id=twin, device_id_type=MESH)
    pl.semaphore_signal(barrier, inc=1, device_id=far, device_id_type=MESH)

    lanes = lax.broadcasted_iota(jnp.int32, (128, PAD), 1)
    rope = jnp.concatenate([rope_ref[...].astype(F32), jnp.zeros((PAD - ROPE, 128), F32)], 0)
    keyf[0] = rope.T
    for b in range(2):
        keyf[b + 1] = lat_ref[:, pl.ds(pl.multiple_of(core * 256 + b * 128, 128), 128)].astype(F32)
    xbuf[...] = jnp.zeros_like(xbuf)
    for t in range(2):
        for q in range(2):
            for jb in range(3):
                xbuf[pl.ds((t * 2 + q) * 3 + jb, 32, stride=16), :] = keyf[
                    jb, pl.ds(t * GROUP + q, 32, stride=2), :
                ]
    send1[...] = xbuf[pl.ds(0, 512), :].astype(BF16).reshape(32, 16, 128)

    sub = lax.broadcasted_iota(jnp.int32, (8, 128), 0)
    cin = lax.broadcasted_iota(jnp.int32, (128, 128), 0)
    cout = lax.broadcasted_iota(jnp.int32, (128, 128), 1)
    reorder = jnp.where(cin == 2 * lax.rem(cout, 64) + lax.div(cout, 64), 1.0, 0.0).astype(BF16)
    plain = jnp.broadcast_to(order_ref[...].astype(F32).reshape(1, 128), (8, 128)).astype(BF16)
    row = dot_nn(plain, reorder)
    zero8 = jnp.zeros((8, 128), F32)

    def fill(n, carry):
        which = lax.div(n, 32)
        group = order_sm[2 * near(lax.rem(n, 32), 1) + which]
        hot = jnp.where(row == (sub + (group - (SPAN - 1))).astype(F32), 1.0, 0.0).astype(F32)
        upper = jnp.concatenate([hot, zero8], 1)
        lower = jnp.concatenate([zero8, hot], 1)
        onehot[pl.ds(pl.multiple_of(n * 16, 16), 16), :] = jnp.concatenate([upper, lower], 0).astype(BF16)
        return carry

    lax.fori_loop(0, 64, fill, 0)
    recvb[...] = jnp.zeros_like(recvb)
    pl.semaphore_wait(barrier, 65)

    pltpu.make_async_copy(send1.at[piece], recv1.at[seq], r1).start()

    def phase1(i, carry):
        dst = around(i)
        pltpu.make_async_remote_copy(
            src_ref=send1.at[piece_of(dst)], dst_ref=recv1.at[seq], send_sem=s1, recv_sem=r1,
            device_id=(dst, head), device_id_type=MESH,
        ).start()
        return carry

    lax.fori_loop(1, 64, phase1, 0)

    for load in loads:
        load.wait()

    def project(h, carry):
        cols = pl.ds(pl.multiple_of(h * NOPE, NOPE), NOPE)
        rows = pl.ds(pl.multiple_of(h * GROUP, GROUP), GROUP)
        ql = dot_nt(qn[:, cols], uk[:, cols]).astype(BF16)
        gl = dot_nt(gout[:, cols], uv[:, cols]).astype(BF16)
        for w in range(2):
            qfull[w, rows, pl.ds(PAD, LATENT)] = ql[w * GROUP:(w + 1) * GROUP]
            glow[w, rows, :] = gl[w * GROUP:(w + 1) * GROUP]
        return carry

    lax.fori_loop(0, HEAD_DEV, project, 0)

    pltpu.make_async_copy(recv1, recv1, r1).wait()
    xbuf[...] = recv1[...].reshape(1024, 128).astype(F32)
    for q in range(2):
        for t in range(2):
            for jb in range(3):
                gather2[(q * 2 + t) * 64:(q * 2 + t + 1) * 64, jb * 128:(jb + 1) * 128] = xbuf[
                    pl.ds((t * 2 + q) * 3 + jb, 64, stride=16), :
                ].astype(BF16)

    def half_of(ref, cr):
        return ref if cr == 0 else ref.at[:, pl.ds(128, 256)]

    def columns(cr):
        return pl.ds(0, 384) if cr == 0 else pl.ds(384, 256)

    def by_core(run):
        for cr in range(2):
            @pl.when(core == cr)
            def _():
                run(cr)

    for which in range(2):
        picked = dot_nn(onehot[which * 512:(which + 1) * 512, :], gather2[...])
        send2[which] = picked.astype(BF16).reshape(32, 16, 384)

        def send_windows(cr):
            pltpu.make_async_copy(
                half_of(send2.at[which, 0], cr), window.at[which, piece, :, columns(cr)], r2.at[which]
            ).start()

            def phase2(o, carry):
                pltpu.make_async_remote_copy(
                    src_ref=half_of(send2.at[which, o], cr), dst_ref=window.at[which, piece, :, columns(cr)],
                    send_sem=s2.at[which], recv_sem=r2.at[which],
                    device_id=(near(o, 1), head), device_id_type=MESH,
                ).start()
                return carry

            lax.fori_loop(1, 32, phase2, 0)

        by_core(send_windows)

    def rotary(m, carry):
        two = qr[:, pl.ds(pl.multiple_of(m * 128, 128), 128)].astype(F32)
        even = jnp.where(lanes < ROPE, two, 0.0).astype(BF16)
        odd = jnp.where(lanes < ROPE, pltpu.roll(two, ROPE, 1), 0.0).astype(BF16)
        for w in range(2):
            qfull[w, pl.ds(pl.multiple_of(m * 128, 128), GROUP), pl.ds(0, PAD)] = even[w * GROUP:(w + 1) * GROUP]
            qfull[w, pl.ds(pl.multiple_of(m * 128 + GROUP, GROUP), GROUP), pl.ds(0, PAD)] = odd[
                w * GROUP:(w + 1) * GROUP
            ]
        return carry

    lax.fori_loop(0, HEAD_DEV // 2, rotary, 0)

    col = lax.broadcasted_iota(jnp.int32, (GROUP, KEYS), 1)
    slot = lax.rem(col, SPAN)
    key_row = lax.div(col, SPAN)
    query_row = lax.broadcasted_iota(jnp.int32, (GROUP, KEYS), 0)
    for which in range(2):
        group = order_sm[2 * seq + which]
        seen = jnp.sum(mask_ref[pl.ds(group, 1), :], axis=1, keepdims=True)
        allowed = (slot >= SPAN - seen) & ((slot < SPAN - 1) | (key_row <= query_row))
        bias[which] = jnp.where(allowed, 0.0, -1e30).astype(F32)

    def cross_copy(src, dst, sem_s, sem_r):
        return pltpu.make_async_remote_copy(
            src_ref=src, dst_ref=dst, send_sem=sem_s, recv_sem=sem_r, device_id=twin, device_id_type=MESH
        )

    for which in range(2):
        onehot_t[which] = onehot[which * 512:(which + 1) * 512, :].T

    def share_window(which):
        def run(cr):
            ref = window.at[which, :, :, columns(cr)]
            pltpu.make_async_copy(ref, ref, r2.at[which]).wait()
            cross_copy(ref, ref, s2c.at[which], r2c.at[which]).start()

        by_core(run)

    def await_window(which):
        def run(cr):
            ref = window.at[which, :, :, columns(1 - cr)]
            pltpu.make_async_copy(ref, ref, r2c.at[which]).wait()

        by_core(run)

    def attend_from(which, first, last):
        def attend(n, carry):
            keys = window[which].reshape(KEYS, WIDTH)
            lat = keys[:, PAD:]
            parts = [pl.ds(pl.multiple_of(n * BLOCK + i * SUB, SUB), SUB) for i in range(BLOCK // SUB)]
            scores = [dot_nt(qfull[which, rows, :], keys) for rows in parts]
            grad_prob = [dot_nt(glow[which, rows, :], lat) for rows in parts]
            for i, rows in enumerate(parts):
                score = scores[i] * SCALE2
                score = (score.reshape(SUB // GROUP, GROUP, KEYS) + bias[which][None]).reshape(SUB, KEYS)
                top = jnp.max(score, axis=1, keepdims=True)
                weights = jnp.exp2(score - top)
                normed = weights * (1.0 / jnp.sum(weights, axis=1, keepdims=True))
                low = normed.astype(BF16)
                probs[rows, :] = low
                ol = dot_nn(low, lat).astype(BF16)
                prod = normed * grad_prob[i]
                delta = jnp.sum(prod, axis=1, keepdims=True)
                ds = (prod - normed * delta).astype(BF16)
                dscore[rows, :] = ds
                gq = (dot_nn(ds, keys) * SCALE).astype(BF16)
                first_head = n * (BLOCK // GROUP) + i * (SUB // GROUP)
                for j in range(SUB // GROUP):
                    part_rows = slice(j * GROUP, (j + 1) * GROUP)
                    olat[first_head + j, which * GROUP:(which + 1) * GROUP, :] = ol[part_rows]
                    gqlat[first_head + j, which * GROUP:(which + 1) * GROUP, :] = gq[part_rows, PAD:]
                for j in range(0, SUB // GROUP, 2):
                    two = jnp.concatenate(
                        [gq[j * GROUP:(j + 1) * GROUP, :ROPE], gq[(j + 1) * GROUP:(j + 2) * GROUP, :ROPE]], 1
                    )
                    gqr_v[
                        which * GROUP:(which + 1) * GROUP,
                        pl.ds(pl.multiple_of(n * BLOCK + i * SUB + j * ROPE, 128), 128),
                    ] = two
            return carry

        lax.fori_loop(first, last, attend, 0)

    def key_grads(which):
        def key_grad(n, carry):
            krows = pl.ds(pl.multiple_of(n * 256, 256), 256)
            first = dot_tn(dscore[:, krows], qfull[which]) * SCALE
            second = dot_tn(probs[:, krows], glow[which])
            total = jnp.concatenate([first[:, :PAD], first[:, PAD:] + second], 1)
            dwin[which, pl.ds(n * 16, 16)] = total.reshape(16, 16, WIDTH)
            return carry

        lax.fori_loop(0, KEYS // 256, key_grad, 0)

    def share_grads(which):
        def run(cr):
            rest = columns(1 - cr)
            into = pl.ds(128, 256) if cr == 0 else pl.ds(0, 384)
            dsend[which, :, :, into] = dwin[which, :, :, rest].astype(BF16)
            cross_copy(
                dsend.at[which, :, :, into], dpair.at[which, :, :, into], s3c.at[which], r3c.at[which]
            ).start()

        by_core(run)

    def send_grads(which):
        def run(cr):
            into = pl.ds(0, 384) if cr == 0 else pl.ds(128, 256)
            ref = dpair.at[which, :, :, into]
            pltpu.make_async_copy(ref, ref, r3c.at[which]).wait()
            dmine[which, :, :, into] = (
                dwin[which, :, :, columns(cr)] + dpair[which, :, :, into].astype(F32)
            ).astype(BF16)
            pltpu.make_async_copy(
                half_of(dmine.at[which, piece], cr), half_of(recvb.at[which, 0], cr), r4.at[which]
            ).start()

            def phase4(i, carry):
                o = 32 - i
                dst = near(o, -1)
                pltpu.make_async_remote_copy(
                    src_ref=half_of(dmine.at[which, piece_of(dst)], cr), dst_ref=half_of(recvb.at[which, o], cr),
                    send_sem=s4.at[which], recv_sem=r4.at[which], device_id=(dst, head), device_id_type=MESH,
                ).start()
                return carry

            lax.fori_loop(1, 32, phase4, 0)

        by_core(run)

    blocks = ROWS // BLOCK
    share_window(0)
    await_window(0)
    attend_from(0, 0, blocks)
    share_window(1)
    key_grads(0)
    share_grads(0)
    await_window(1)
    attend_from(1, 0, 1)
    send_grads(0)
    attend_from(1, 1, blocks)
    key_grads(1)
    share_grads(1)
    send_grads(1)

    def unproject(h, carry):
        cols = pl.ds(pl.multiple_of(h * NOPE, NOPE), NOPE)
        out_v[:, cols] = dot_nn(olat[h], uv[:, cols]).astype(BF16)
        gqn_v[:, cols] = dot_nn(gqlat[h], uk[:, cols]).astype(BF16)
        return carry

    lax.fori_loop(0, HEAD_DEV, unproject, 0)
    stores = [
        pltpu.make_async_copy(src, dst, outsem.at[n])
        for n, (src, dst) in enumerate([(out_v, out_hbm), (gqn_v, gqn_hbm), (gqr_v, gqr_hbm)])
    ]
    for store in stores:
        store.start()

    total = jnp.zeros((256, 384), F32)
    for which in range(2):
        def await_grads(cr):
            ref = recvb.at[which] if cr == 0 else recvb.at[which, :, :, pl.ds(128, 256)]
            pltpu.make_async_copy(ref, ref, r4.at[which]).wait()

        by_core(await_grads)
        total = total + dot_nn(onehot_t[which], recvb[which].reshape(512, 384))
    for q in range(2):
        for t in range(2):
            for jb in range(3):
                xbuf[pl.ds((t * 2 + q) * 3 + jb, 64, stride=16), :] = total[
                    (q * 2 + t) * 64:(q * 2 + t + 1) * 64, jb * 128:(jb + 1) * 128
                ]
    send7[...] = xbuf[...].astype(BF16).reshape(64, 16, 128)

    pltpu.make_async_copy(send7.at[seq], recv7.at[plane, piece], r7).start()

    def phase7(i, carry):
        dst = around(i)
        pltpu.make_async_remote_copy(
            src_ref=send7.at[dst], dst_ref=recv7.at[plane, piece], send_sem=s7, recv_sem=r7,
            device_id=(dst, head), device_id_type=MESH,
        ).start()
        return carry

    lax.fori_loop(1, 64, phase7, 0)
    pltpu.make_async_copy(recv7, recv7, r7).wait()
    xbuf[pl.ds(0, 512), :] = (recv7[0].astype(F32) + recv7[1].astype(F32)).reshape(512, 128)
    for t in range(2):
        for q in range(2):
            for jb in range(3):
                keyf[jb, pl.ds(t * GROUP + q, 32, stride=2), :] = xbuf[
                    pl.ds((t * 2 + q) * 3 + jb, 32, stride=16), :
                ]
    part[...] = keyf[...].astype(BF16)

    def add_far(cr):
        blocks3 = pl.ds(0, 3) if cr == 0 else pl.ds(1, 2)
        mine = pl.ds(0, 3) if cr == 0 else pl.ds(3, 2)
        rest = pl.ds(3, 2) if cr == 0 else pl.ds(0, 3)
        copy = pltpu.make_async_remote_copy(
            src_ref=part.at[blocks3], dst_ref=fpart.at[blocks3], send_sem=s8, recv_sem=r8,
            device_id=far, device_id_type=MESH,
        )
        copy.start()
        copy.wait_recv()
        home[mine] = (part[blocks3].astype(F32) + fpart[blocks3].astype(F32)).astype(BF16)
        cross_copy(home.at[mine], home.at[mine], s9, r9).start()
        pltpu.make_async_copy(home.at[rest], home.at[rest], r9).wait()
        copy.wait_send()
        pltpu.make_async_copy(home.at[mine], home.at[mine], s9).wait()

    by_core(add_far)
    for b in range(4):
        glat_ref[:, b * 128:(b + 1) * 128] = home[b + 1]
    grope_ref[...] = home[0].astype(F32).T[:ROPE].astype(BF16)

    def drain(ref, sem):
        pltpu.make_async_copy(ref, ref, sem).wait()

    drain(recv1.at[pl.ds(0, 63)], s1)
    drain(send7.at[pl.ds(0, 63)], s7)

    def drain_halves(cr):
        for which in range(2):
            own = pl.ds(0, 384) if cr == 0 else pl.ds(128, 256)
            rest = pl.ds(128, 256) if cr == 0 else pl.ds(0, 384)
            drain(send2.at[which, pl.ds(0, 31), :, own], s2.at[which])
            drain(dmine.at[which, pl.ds(0, 31), :, own], s4.at[which])
            drain(window.at[which, :, :, columns(cr)], s2c.at[which])
            drain(dsend.at[which, :, :, rest], s3c.at[which])

    by_core(drain_halves)
    for store in stores:
        store.wait()


def copy_kernel(*refs):
    count = (len(refs) - 2) // 3
    srcs, dsts, held = refs[:count], refs[count:2 * count], refs[2 * count:3 * count]
    insem, outsem = refs[3 * count:]
    reads = [pltpu.make_async_copy(srcs[n], held[n], insem.at[n]) for n in range(count)]
    writes = [pltpu.make_async_copy(held[n], dsts[n], outsem.at[n]) for n in range(count)]
    for read in reads:
        read.start()
    for read, write in zip(reads, writes):
        read.wait()
        write.start()
    for write in writes:
        write.wait()


def local(
    query_nope, query_rope, latent, key_rope, up_key, up_value, grad_out, group_order, tile_mask
):
    vmem = pl.BlockSpec(memory_space=pltpu.VMEM)
    smem = pl.BlockSpec(memory_space=pltpu.SMEM)
    hbm = pl.BlockSpec(memory_space=pl.ANY)
    dma = pltpu.SemaphoreType.DMA
    scratch = [
        pltpu.VMEM((128, 2048), BF16),
        pltpu.VMEM((128, 1024), BF16),
        pltpu.VMEM((LATENT, 2048), BF16),
        pltpu.VMEM((LATENT, 2048), BF16),
        pltpu.VMEM((128, 2048), BF16),
        pltpu.VMEM((128, 128), jnp.int32),
        pltpu.VMEM((128, 2048), BF16),
        pltpu.VMEM((128, 2048), BF16),
        pltpu.VMEM((128, 1024), BF16),
        pltpu.VMEM((3, 128, 128), F32),
        pltpu.VMEM((1024, 128), F32),
        pltpu.VMEM((32, 16, 128), BF16),
        pltpu.VMEM((64, 16, 128), BF16),
        pltpu.VMEM((256, 384), BF16),
        pltpu.VMEM((1024, 256), BF16),
        pltpu.VMEM((2, 32, 16, 384), BF16),
        pltpu.VMEM((2, 32, 16, WIDTH), BF16),
        pltpu.VMEM((2, ROWS, WIDTH), BF16),
        pltpu.VMEM((2, ROWS, LATENT), BF16),
        pltpu.VMEM((HEAD_DEV, 128, LATENT), BF16),
        pltpu.VMEM((HEAD_DEV, 128, LATENT), BF16),
        pltpu.VMEM((ROWS, KEYS), BF16),
        pltpu.VMEM((ROWS, KEYS), BF16),
        pltpu.VMEM((2, GROUP, KEYS), F32),
        pltpu.VMEM((2, 32, 16, WIDTH), F32),
        pltpu.VMEM((2, 32, 16, 384), BF16),
        pltpu.VMEM((2, 32, 16, 384), BF16),
        pltpu.VMEM((2, 32, 16, 384), BF16),
        pltpu.VMEM((2, 32, 16, 384), BF16),
        pltpu.VMEM((2, 256, 512), BF16),
        pltpu.VMEM((64, 16, 128), BF16),
        pltpu.VMEM((2, 32, 16, 128), BF16),
        pltpu.VMEM((3, 128, 128), BF16),
        pltpu.VMEM((3, 128, 128), BF16),
        pltpu.VMEM((5, 128, 128), BF16),
        dma((6,)), dma((3,)),
        dma, dma,
        dma((2,)), dma((2,)), dma((2,)), dma((2,)),
        dma((2,)), dma((2,)),
        dma((2,)), dma((2,)),
        dma, dma, dma, dma, dma, dma,
    ]
    shapes = (
        jax.ShapeDtypeStruct((128, 2048), BF16),
        jax.ShapeDtypeStruct((128, 2048), BF16),
        jax.ShapeDtypeStruct((128, 1024), BF16),
        jax.ShapeDtypeStruct((128, LATENT), BF16),
        jax.ShapeDtypeStruct((ROPE, 128), BF16),
    )
    results = pl.pallas_call(
        kernel,
        out_shape=shapes,
        in_specs=[hbm, hbm, vmem, vmem, hbm, hbm, hbm, smem, vmem, hbm],
        out_specs=(hbm, hbm, hbm, vmem, vmem),
        scratch_shapes=scratch,
        compiler_params=pltpu.CompilerParams(
            collective_id=0, has_side_effects=True, vmem_limit_bytes=56 << 20
        ),
    )(
        query_nope, query_rope, latent, key_rope.T, up_key, up_value, grad_out,
        group_order, group_order, tile_mask,
    )
    out, gqn, gqr, glat, grope = pl.pallas_call(
        copy_kernel,
        out_shape=shapes,
        in_specs=[hbm] * 5,
        out_specs=(hbm,) * 5,
        scratch_shapes=[pltpu.VMEM(a.shape, a.dtype) for a in shapes] + [dma((5,)), dma((5,))],
    )(*results)
    return out, gqn, gqr, glat, grope.T


def solution(mesh):
    placed = (
        P("seq", "head"),
        P("seq", "head"),
        P("seq", None),
        P("seq", None),
        P(None, "head"),
        P(None, "head"),
        P("seq", "head"),
        P(),
        P(),
    )
    return jax.shard_map(
        local,
        mesh=mesh,
        in_specs=placed,
        out_specs=(
            P("seq", "head"),
            P("seq", "head"),
            P("seq", "head"),
            P("seq", None),
            P("seq", None),
        ),
        check_vma=False,
    )
```

```python
import functools
import math

import jax
import jax.numpy as jnp
from jax import lax
from jax.experimental import pallas as pl
from jax.experimental.pallas import tpu as pltpu
from jax.sharding import PartitionSpec as P

HEAD_DEV = 16
LATENT = 512
ROPE = 64
NOPE = 128
SPAN = 8
GROUP = 64
PAD = 128
WIDTH = PAD + LATENT
KEYS = SPAN * GROUP
ROWS = HEAD_DEV * GROUP
MESH = pl.DeviceIdType.MESH
SCALE = (NOPE + ROPE) ** (-0.5)
SCALE2 = SCALE * math.log2(math.e)
BLOCK = 512
SUB = 256
F32 = jnp.float32
BF16 = jnp.bfloat16


def dot_nt(a, b):
    return lax.dot_general(a, b, (((1,), (1,)), ((), ())), preferred_element_type=F32)


def dot_nn(a, b):
    return lax.dot_general(a, b, (((1,), (0,)), ((), ())), preferred_element_type=F32)


def dot_tn(a, b):
    return lax.dot_general(a, b, (((0,), (0,)), ((), ())), preferred_element_type=F32)


def kernel(
    qn_hbm, qr_hbm, lat_hbm, rope_hbm, uk_hbm, uv_hbm, go_hbm, order_hbm, mask_hbm,
    out_hbm, gqn_hbm, gqr_hbm, glat_ref, grope_ref,
    lat_ref, rope_ref, order_sm, order_ref, qn, qr, uk, uv, gout, mask_ref, out_v, gqn_v, gqr_v,
    keyf, xbuf, send1, recv1, gather2, onehot, send2, window,
    qfull, glow, olat, gqlat, probs, dscore, bias,
    dwin, dsend, dpair, dmine, recvb, onehot_t, send7, recv7, home,
    insem, outsem, s1, r1, s2, r2, s2c, r2c,
    s3c, r3c, s4, r4, s7, r7, s9, r9,
):
    seq = lax.axis_index("seq")
    head = lax.axis_index("head")
    core = lax.rem(head, 2)
    x = lax.div(seq, 16)
    z = lax.rem(lax.div(seq, 2), 8)
    y = lax.rem(seq, 2)
    plane = lax.div(z, 4)
    piece = x * 8 + lax.rem(z, 4) * 2 + y
    twin = (seq, head + 1 - 2 * core)
    far = (seq, lax.rem(head + 2, 4))
    far_twin = (seq, lax.rem(head + 3 - 2 * core, 4))

    def around(i):
        return lax.rem(seq + i, 64)

    def piece_of(device):
        return lax.div(device, 16) * 8 + lax.rem(lax.div(device, 2), 4) * 2 + lax.rem(device, 2)

    def near(o, sign):
        step = lax.div(o, 8)
        shift = step + 5 * lax.div(step, 2) - 6 * lax.div(step, 3) + 4 * core * lax.div(step, 3)
        xo = lax.rem(lax.div(o, 2), 4)
        nx = lax.rem(x + 4 + sign * xo, 4)
        nz = lax.rem(z + 8 + sign * shift, 8)
        ny = lax.rem(y + lax.rem(o, 2), 2)
        return nx * 16 + nz * 2 + ny

    barrier = pltpu.get_barrier_semaphore()

    def greet(i, carry):
        pl.semaphore_signal(barrier, inc=1, device_id=(around(i), head), device_id_type=MESH)
        return carry

    lax.fori_loop(1, 64, greet, 0)
    pl.semaphore_signal(barrier, inc=1, device_id=twin, device_id_type=MESH)
    pl.semaphore_signal(barrier, inc=1, device_id=far, device_id_type=MESH)
    pl.semaphore_signal(barrier, inc=1, device_id=far_twin, device_id_type=MESH)

    early = [
        pltpu.make_async_copy(src, dst, insem.at[n])
        for n, (src, dst) in enumerate(
            [(lat_hbm, lat_ref), (rope_hbm, rope_ref), (order_hbm, order_ref), (order_hbm, order_sm)]
        )
    ]
    for load in early:
        load.start()
    loads = [
        pltpu.make_async_copy(src, dst, insem.at[4 + n])
        for n, (src, dst) in enumerate(
            [(qn_hbm, qn), (qr_hbm, qr), (uk_hbm, uk), (uv_hbm, uv), (go_hbm, gout), (mask_hbm, mask_ref)]
        )
    ]
    for load in loads:
        load.start()

    for load in early:
        load.wait()

    lanes = lax.broadcasted_iota(jnp.int32, (128, PAD), 1)
    rope = jnp.concatenate([rope_ref[...].astype(F32), jnp.zeros((PAD - ROPE, 128), F32)], 0)
    keyf[0] = rope.T
    for b in range(2):
        keyf[b + 1] = lat_ref[:, pl.ds(pl.multiple_of(core * 256 + b * 128, 128), 128)].astype(F32)
    xbuf[...] = jnp.zeros_like(xbuf)
    for t in range(2):
        for q in range(2):
            for jb in range(3):
                xbuf[pl.ds((t * 2 + q) * 3 + jb, 32, stride=16), :] = keyf[
                    jb, pl.ds(t * GROUP + q, 32, stride=2), :
                ]
    send1[...] = xbuf[pl.ds(0, 512), :].astype(BF16).reshape(32, 16, 128)

    sub = lax.broadcasted_iota(jnp.int32, (8, 128), 0)
    cin = lax.broadcasted_iota(jnp.int32, (128, 128), 0)
    cout = lax.broadcasted_iota(jnp.int32, (128, 128), 1)
    reorder = jnp.where(cin == 2 * lax.rem(cout, 64) + lax.div(cout, 64), 1.0, 0.0).astype(BF16)
    plain = jnp.broadcast_to(order_ref[...].astype(F32).reshape(1, 128), (8, 128)).astype(BF16)
    row = dot_nn(plain, reorder)
    zero8 = jnp.zeros((8, 128), F32)

    def fill(n, carry):
        which = lax.div(n, 32)
        group = order_sm[2 * near(lax.rem(n, 32), 1) + which]
        hot = jnp.where(row == (sub + (group - (SPAN - 1))).astype(F32), 1.0, 0.0).astype(F32)
        upper = jnp.concatenate([hot, zero8], 1)
        lower = jnp.concatenate([zero8, hot], 1)
        onehot[pl.ds(pl.multiple_of(n * 16, 16), 16), :] = jnp.concatenate([upper, lower], 0).astype(BF16)
        return carry

    lax.fori_loop(0, 64, fill, 0)
    recvb[...] = jnp.zeros_like(recvb)
    pl.semaphore_wait(barrier, 66)

    pltpu.make_async_copy(send1.at[piece], recv1.at[seq], r1).start()

    def phase1(i, carry):
        dst = around(i)
        pltpu.make_async_remote_copy(
            src_ref=send1.at[piece_of(dst)], dst_ref=recv1.at[seq], send_sem=s1, recv_sem=r1,
            device_id=(dst, head), device_id_type=MESH,
        ).start()
        return carry

    lax.fori_loop(1, 64, phase1, 0)

    for load in loads:
        load.wait()

    def project(h, carry):
        cols = pl.ds(pl.multiple_of(h * NOPE, NOPE), NOPE)
        rows = pl.ds(pl.multiple_of(h * GROUP, GROUP), GROUP)
        ql = dot_nt(qn[:, cols], uk[:, cols]).astype(BF16)
        gl = dot_nt(gout[:, cols], uv[:, cols]).astype(BF16)
        for w in range(2):
            qfull[w, rows, pl.ds(PAD, LATENT)] = ql[w * GROUP:(w + 1) * GROUP]
            glow[w, rows, :] = gl[w * GROUP:(w + 1) * GROUP]
        return carry

    lax.fori_loop(0, HEAD_DEV, project, 0)

    pltpu.make_async_copy(recv1, recv1, r1).wait()
    xbuf[...] = recv1[...].reshape(1024, 128).astype(F32)
    for q in range(2):
        for t in range(2):
            for jb in range(3):
                gather2[(q * 2 + t) * 64:(q * 2 + t + 1) * 64, jb * 128:(jb + 1) * 128] = xbuf[
                    pl.ds((t * 2 + q) * 3 + jb, 64, stride=16), :
                ].astype(BF16)

    def half_of(ref, cr):
        return ref if cr == 0 else ref.at[:, pl.ds(128, 256)]

    def columns(cr):
        return pl.ds(0, 384) if cr == 0 else pl.ds(384, 256)

    def by_core(run):
        for cr in range(2):
            @pl.when(core == cr)
            def _():
                run(cr)

    for which in range(2):
        picked = dot_nn(onehot[which * 512:(which + 1) * 512, :], gather2[...])
        send2[which] = picked.astype(BF16).reshape(32, 16, 384)

        def send_windows(cr):
            pltpu.make_async_copy(
                half_of(send2.at[which, 0], cr), window.at[which, piece, :, columns(cr)], r2.at[which]
            ).start()

            def phase2(o, carry):
                pltpu.make_async_remote_copy(
                    src_ref=half_of(send2.at[which, o], cr), dst_ref=window.at[which, piece, :, columns(cr)],
                    send_sem=s2.at[which], recv_sem=r2.at[which],
                    device_id=(near(o, 1), head), device_id_type=MESH,
                ).start()
                return carry

            lax.fori_loop(1, 32, phase2, 0)

        by_core(send_windows)

    def rotary(m, carry):
        two = qr[:, pl.ds(pl.multiple_of(m * 128, 128), 128)].astype(F32)
        even = jnp.where(lanes < ROPE, two, 0.0).astype(BF16)
        odd = jnp.where(lanes < ROPE, pltpu.roll(two, ROPE, 1), 0.0).astype(BF16)
        for w in range(2):
            qfull[w, pl.ds(pl.multiple_of(m * 128, 128), GROUP), pl.ds(0, PAD)] = even[w * GROUP:(w + 1) * GROUP]
            qfull[w, pl.ds(pl.multiple_of(m * 128 + GROUP, GROUP), GROUP), pl.ds(0, PAD)] = odd[
                w * GROUP:(w + 1) * GROUP
            ]
        return carry

    lax.fori_loop(0, HEAD_DEV // 2, rotary, 0)

    col = lax.broadcasted_iota(jnp.int32, (GROUP, KEYS), 1)
    slot = lax.rem(col, SPAN)
    key_row = lax.div(col, SPAN)
    query_row = lax.broadcasted_iota(jnp.int32, (GROUP, KEYS), 0)
    for which in range(2):
        group = order_sm[2 * seq + which]
        seen = jnp.sum(mask_ref[pl.ds(group, 1), :], axis=1, keepdims=True)
        allowed = (slot >= SPAN - seen) & ((slot < SPAN - 1) | (key_row <= query_row))
        bias[which] = jnp.where(allowed, 0.0, -1e30).astype(F32)

    def cross_copy(src, dst, sem_s, sem_r):
        return pltpu.make_async_remote_copy(
            src_ref=src, dst_ref=dst, send_sem=sem_s, recv_sem=sem_r, device_id=twin, device_id_type=MESH
        )

    for which in range(2):
        onehot_t[which] = onehot[which * 512:(which + 1) * 512, :].T

    def share_window(which):
        def run(cr):
            ref = window.at[which, :, :, columns(cr)]
            pltpu.make_async_copy(ref, ref, r2.at[which]).wait()
            cross_copy(ref, ref, s2c.at[which], r2c.at[which]).start()

        by_core(run)

    def await_window(which):
        def run(cr):
            ref = window.at[which, :, :, columns(1 - cr)]
            pltpu.make_async_copy(ref, ref, r2c.at[which]).wait()

        by_core(run)

    def attend_from(which, first, last):
        def attend(n, carry):
            keys = window[which].reshape(KEYS, WIDTH)
            lat = keys[:, PAD:]
            parts = [pl.ds(pl.multiple_of(n * BLOCK + i * SUB, SUB), SUB) for i in range(BLOCK // SUB)]
            scores = [dot_nt(qfull[which, rows, :], keys) for rows in parts]
            grad_prob = [dot_nt(glow[which, rows, :], lat) for rows in parts]
            for i, rows in enumerate(parts):
                score = scores[i] * SCALE2
                score = (score.reshape(SUB // GROUP, GROUP, KEYS) + bias[which][None]).reshape(SUB, KEYS)
                top = jnp.max(score, axis=1, keepdims=True)
                weights = jnp.exp2(score - top)
                normed = weights * (1.0 / jnp.sum(weights, axis=1, keepdims=True))
                low = normed.astype(BF16)
                probs[rows, :] = low
                ol = dot_nn(low, lat).astype(BF16)
                prod = normed * grad_prob[i]
                delta = jnp.sum(prod, axis=1, keepdims=True)
                ds = (prod - normed * delta).astype(BF16)
                dscore[rows, :] = ds
                gq = (dot_nn(ds, keys) * SCALE).astype(BF16)
                first_head = n * (BLOCK // GROUP) + i * (SUB // GROUP)
                for j in range(SUB // GROUP):
                    part_rows = slice(j * GROUP, (j + 1) * GROUP)
                    olat[first_head + j, which * GROUP:(which + 1) * GROUP, :] = ol[part_rows]
                    gqlat[first_head + j, which * GROUP:(which + 1) * GROUP, :] = gq[part_rows, PAD:]
                for j in range(0, SUB // GROUP, 2):
                    two = jnp.concatenate(
                        [gq[j * GROUP:(j + 1) * GROUP, :ROPE], gq[(j + 1) * GROUP:(j + 2) * GROUP, :ROPE]], 1
                    )
                    gqr_v[
                        which * GROUP:(which + 1) * GROUP,
                        pl.ds(pl.multiple_of(n * BLOCK + i * SUB + j * ROPE, 128), 128),
                    ] = two
            return carry

        lax.fori_loop(first, last, attend, 0)

    def key_grads(which, h):
        krows = slice(h * 256, (h + 1) * 256)
        first = dot_tn(dscore[:, krows], qfull[which]) * SCALE
        second = dot_tn(probs[:, krows], glow[which])
        total = jnp.concatenate([first[:, :PAD], first[:, PAD:] + second], 1)
        dwin[which, h * 16:(h + 1) * 16] = total.reshape(16, 16, WIDTH)

    def share_grads(which, h):
        some = pl.ds(h * 16, 16)

        def run(cr):
            rest = columns(1 - cr)
            into = pl.ds(128, 256) if cr == 0 else pl.ds(0, 384)
            dsend[which, some, :, into] = dwin[which, some, :, rest].astype(BF16)
            cross_copy(
                dsend.at[which, some, :, into], dpair.at[which, some, :, into],
                s3c.at[2 * which + h], r3c.at[2 * which + h],
            ).start()

        by_core(run)

    def send_grads(which, h):
        some = pl.ds(h * 16, 16)

        def run(cr):
            into = pl.ds(0, 384) if cr == 0 else pl.ds(128, 256)
            ref = dpair.at[which, some, :, into]
            pltpu.make_async_copy(ref, ref, r3c.at[2 * which + h]).wait()
            dmine[which, some, :, into] = (
                dwin[which, some, :, columns(cr)] + dpair[which, some, :, into].astype(F32)
            ).astype(BF16)

            def phase4(i, carry):
                xo = lax.rem(x + 4 - (2 * h + lax.rem(lax.div(i, 2), 2)), 4)
                o = (3 - lax.div(i, 4)) * 8 + xo * 2 + lax.rem(i, 2)
                dst = near(o, -1)
                src_ref = half_of(dmine.at[which, piece_of(dst)], cr)
                dst_ref = half_of(recvb.at[which, o], cr)

                @pl.when(o == 0)
                def _():
                    pltpu.make_async_copy(src_ref, dst_ref, r4.at[which]).start()

                @pl.when(o != 0)
                def _():
                    pltpu.make_async_remote_copy(
                        src_ref=src_ref, dst_ref=dst_ref, send_sem=s4.at[which], recv_sem=r4.at[which],
                        device_id=(dst, head), device_id_type=MESH,
                    ).start()

                return carry

            lax.fori_loop(0, 16, phase4, 0)

        by_core(run)

    blocks = ROWS // BLOCK
    share_window(0)
    await_window(0)
    attend_from(0, 0, blocks)
    share_window(1)
    for h in range(2):
        key_grads(0, h)
        share_grads(0, h)
    await_window(1)
    attend_from(1, 0, 1)
    for h in range(2):
        send_grads(0, h)
    attend_from(1, 1, blocks)
    for h in range(2):
        key_grads(1, h)
        share_grads(1, h)
    for h in range(2):
        send_grads(1, h)

    def unproject(h, carry):
        cols = pl.ds(pl.multiple_of(h * NOPE, NOPE), NOPE)
        out_v[:, cols] = dot_nn(olat[h], uv[:, cols]).astype(BF16)
        gqn_v[:, cols] = dot_nn(gqlat[h], uk[:, cols]).astype(BF16)
        return carry

    lax.fori_loop(0, HEAD_DEV, unproject, 0)
    stores = [
        pltpu.make_async_copy(src, dst, outsem.at[n])
        for n, (src, dst) in enumerate([(out_v, out_hbm), (gqn_v, gqn_hbm), (gqr_v, gqr_hbm)])
    ]
    for store in stores:
        store.start()

    total = jnp.zeros((256, 384), F32)
    for which in range(2):
        def await_grads(cr):
            ref = recvb.at[which] if cr == 0 else recvb.at[which, :, :, pl.ds(128, 256)]
            pltpu.make_async_copy(ref, ref, r4.at[which]).wait()

        by_core(await_grads)
        total = total + dot_nn(onehot_t[which], recvb[which].reshape(512, 384))
    for q in range(2):
        for t in range(2):
            for jb in range(3):
                xbuf[pl.ds((t * 2 + q) * 3 + jb, 64, stride=16), :] = total[
                    (q * 2 + t) * 64:(q * 2 + t + 1) * 64, jb * 128:(jb + 1) * 128
                ]
    send7[...] = xbuf[...].astype(BF16).reshape(64, 16, 128)

    pltpu.make_async_copy(send7.at[seq], recv7.at[plane, piece], r7).start()

    def phase7(i, carry):
        dst = around(i)
        pltpu.make_async_remote_copy(
            src_ref=send7.at[dst], dst_ref=recv7.at[plane, piece], send_sem=s7, recv_sem=r7,
            device_id=(dst, head), device_id_type=MESH,
        ).start()
        return carry

    lax.fori_loop(1, 64, phase7, 0)
    pltpu.make_async_copy(recv7, recv7, r7).wait()
    xbuf[pl.ds(0, 512), :] = (recv7[0].astype(F32) + recv7[1].astype(F32)).reshape(512, 128)
    for t in range(2):
        for q in range(2):
            for jb in range(3):
                keyf[jb, pl.ds(t * GROUP + q, 32, stride=2), :] = xbuf[
                    pl.ds((t * 2 + q) * 3 + jb, 32, stride=16), :
                ]
    home[pl.ds(head * 3, 3)] = keyf[...].astype(BF16)

    def send_home(cr):
        ref = home.at[pl.ds(head * 3 + cr, 3 - cr)]
        for dst in (far, far_twin, twin):
            pltpu.make_async_remote_copy(
                src_ref=ref, dst_ref=ref, send_sem=s9, recv_sem=r9, device_id=dst, device_id_type=MESH
            ).start()
        got = home.at[pl.ds(0, 7 + cr)]
        pltpu.make_async_copy(got, got, r9).wait()

    by_core(send_home)

    def both(block):
        return home[block].astype(F32) + home[block + 6].astype(F32)

    for b in range(4):
        glat_ref[:, b * 128:(b + 1) * 128] = both(b // 2 * 3 + b % 2 + 1).astype(BF16)
    grope_ref[...] = both(0).T[:ROPE].astype(BF16)

    def drain(ref, sem):
        pltpu.make_async_copy(ref, ref, sem).wait()

    drain(recv1.at[pl.ds(0, 63)], s1)
    drain(send7.at[pl.ds(0, 63)], s7)

    def drain_halves(cr):
        for which in range(2):
            own = pl.ds(0, 384) if cr == 0 else pl.ds(128, 256)
            rest = pl.ds(128, 256) if cr == 0 else pl.ds(0, 384)
            drain(send2.at[which, pl.ds(0, 31), :, own], s2.at[which])
            drain(dmine.at[which, pl.ds(0, 31), :, own], s4.at[which])
            drain(window.at[which, :, :, columns(cr)], s2c.at[which])
            for h in range(2):
                drain(dsend.at[which, pl.ds(h * 16, 16), :, rest], s3c.at[2 * which + h])

    by_core(drain_halves)

    def drain_home(cr):
        ref = home.at[pl.ds(0, 3 * (3 - cr))]
        drain(ref, s9)

    by_core(drain_home)
    for store in stores:
        store.wait()


def copy_kernel(*refs):
    count = (len(refs) - 2) // 3
    srcs, dsts, held = refs[:count], refs[count:2 * count], refs[2 * count:3 * count]
    insem, outsem = refs[3 * count:]
    reads = [pltpu.make_async_copy(srcs[n], held[n], insem.at[n]) for n in range(count)]
    writes = [pltpu.make_async_copy(held[n], dsts[n], outsem.at[n]) for n in range(count)]
    for read in reads:
        read.start()
    for read, write in zip(reads, writes):
        read.wait()
        write.start()
    for write in writes:
        write.wait()


def local(
    query_nope, query_rope, latent, key_rope, up_key, up_value, grad_out, group_order, tile_mask
):
    vmem = pl.BlockSpec(memory_space=pltpu.VMEM)
    hbm = pl.BlockSpec(memory_space=pl.ANY)
    dma = pltpu.SemaphoreType.DMA
    scratch = [
        pltpu.VMEM((128, LATENT), BF16),
        pltpu.VMEM((ROPE, 128), BF16),
        pltpu.SMEM((128,), jnp.int32),
        pltpu.VMEM((128,), jnp.int32),
        pltpu.VMEM((128, 2048), BF16),
        pltpu.VMEM((128, 1024), BF16),
        pltpu.VMEM((LATENT, 2048), BF16),
        pltpu.VMEM((LATENT, 2048), BF16),
        pltpu.VMEM((128, 2048), BF16),
        pltpu.VMEM((128, 128), jnp.int32),
        pltpu.VMEM((128, 2048), BF16),
        pltpu.VMEM((128, 2048), BF16),
        pltpu.VMEM((128, 1024), BF16),
        pltpu.VMEM((3, 128, 128), F32),
        pltpu.VMEM((1024, 128), F32),
        pltpu.VMEM((32, 16, 128), BF16),
        pltpu.VMEM((64, 16, 128), BF16),
        pltpu.VMEM((256, 384), BF16),
        pltpu.VMEM((1024, 256), BF16),
        pltpu.VMEM((2, 32, 16, 384), BF16),
        pltpu.VMEM((2, 32, 16, WIDTH), BF16),
        pltpu.VMEM((2, ROWS, WIDTH), BF16),
        pltpu.VMEM((2, ROWS, LATENT), BF16),
        pltpu.VMEM((HEAD_DEV, 128, LATENT), BF16),
        pltpu.VMEM((HEAD_DEV, 128, LATENT), BF16),
        pltpu.VMEM((ROWS, KEYS), BF16),
        pltpu.VMEM((ROWS, KEYS), BF16),
        pltpu.VMEM((2, GROUP, KEYS), F32),
        pltpu.VMEM((2, 32, 16, WIDTH), F32),
        pltpu.VMEM((2, 32, 16, 384), BF16),
        pltpu.VMEM((2, 32, 16, 384), BF16),
        pltpu.VMEM((2, 32, 16, 384), BF16),
        pltpu.VMEM((2, 32, 16, 384), BF16),
        pltpu.VMEM((2, 256, 512), BF16),
        pltpu.VMEM((64, 16, 128), BF16),
        pltpu.VMEM((2, 32, 16, 128), BF16),
        pltpu.VMEM((12, 128, 128), BF16),
        dma((10,)), dma((3,)),
        dma, dma,
        dma((2,)), dma((2,)), dma((2,)), dma((2,)),
        dma((4,)), dma((4,)),
        dma((2,)), dma((2,)),
        dma, dma, dma, dma,
    ]
    shapes = (
        jax.ShapeDtypeStruct((128, 2048), BF16),
        jax.ShapeDtypeStruct((128, 2048), BF16),
        jax.ShapeDtypeStruct((128, 1024), BF16),
        jax.ShapeDtypeStruct((128, LATENT), BF16),
        jax.ShapeDtypeStruct((ROPE, 128), BF16),
    )
    results = pl.pallas_call(
        kernel,
        out_shape=shapes,
        in_specs=[hbm] * 9,
        out_specs=(hbm, hbm, hbm, vmem, vmem),
        scratch_shapes=scratch,
        compiler_params=pltpu.CompilerParams(
            collective_id=0, has_side_effects=True, vmem_limit_bytes=56 << 20
        ),
    )(
        query_nope, query_rope, latent, key_rope.T, up_key, up_value, grad_out,
        group_order, tile_mask,
    )
    out, gqn, gqr, glat, grope = pl.pallas_call(
        copy_kernel,
        out_shape=shapes,
        in_specs=[hbm] * 5,
        out_specs=(hbm,) * 5,
        scratch_shapes=[pltpu.VMEM(a.shape, a.dtype) for a in shapes] + [dma((5,)), dma((5,))],
    )(*results)
    return out, gqn, gqr, glat, grope.T


def solution(mesh):
    placed = (
        P("seq", "head"),
        P("seq", "head"),
        P("seq", None),
        P("seq", None),
        P(None, "head"),
        P(None, "head"),
        P("seq", "head"),
        P(),
        P(),
    )
    return jax.shard_map(
        local,
        mesh=mesh,
        in_specs=placed,
        out_specs=(
            P("seq", "head"),
            P("seq", "head"),
            P("seq", "head"),
            P("seq", None),
            P("seq", None),
        ),
        check_vma=False,
    )
```

```python
import functools
import math

import jax
import jax.numpy as jnp
from jax import lax
from jax.experimental import pallas as pl
from jax.experimental.pallas import tpu as pltpu
from jax.sharding import PartitionSpec as P

HEAD_DEV = 16
LATENT = 512
ROPE = 64
NOPE = 128
SPAN = 8
GROUP = 64
PAD = 128
WIDTH = PAD + LATENT
KEYS = SPAN * GROUP
ROWS = HEAD_DEV * GROUP
MESH = pl.DeviceIdType.MESH
SCALE = (NOPE + ROPE) ** (-0.5)
SCALE2 = SCALE * math.log2(math.e)
BLOCK = 512
SUB = 256
F32 = jnp.float32
BF16 = jnp.bfloat16


def dot_nt(a, b):
    return lax.dot_general(a, b, (((1,), (1,)), ((), ())), preferred_element_type=F32)


def dot_nn(a, b):
    return lax.dot_general(a, b, (((1,), (0,)), ((), ())), preferred_element_type=F32)


def dot_tn(a, b):
    return lax.dot_general(a, b, (((0,), (0,)), ((), ())), preferred_element_type=F32)


def kernel(
    qn_hbm, qr_hbm, lat_hbm, rope_hbm, uk_hbm, uv_hbm, go_hbm, order_hbm, mask_hbm,
    out_hbm, gqn_hbm, gqr_hbm, glat_ref, grope_ref,
    lat_ref, rope_ref, order_sm, order_ref, qn, qr, uk, uv, gout, mask_ref, out_v, gqn_v, gqr_v,
    keyf, xbuf, send1, recv1, gather2, onehot, send2, window,
    qfull, glow, olat, gqlat, probs, dscore, bias,
    dwin, dsend, dpair, dmine, recvb, onehot_t, send7, recv7, home,
    insem, outsem, s1, r1, s2, r2, s2c, r2c,
    s3c, r3c, s4, r4, s7, r7, s9, r9,
):
    seq = lax.axis_index("seq")
    head = lax.axis_index("head")
    core = lax.rem(head, 2)
    x = lax.div(seq, 16)
    z = lax.rem(lax.div(seq, 2), 8)
    y = lax.rem(seq, 2)
    plane = lax.div(z, 4)
    piece = x * 8 + lax.rem(z, 4) * 2 + y
    twin = (seq, head + 1 - 2 * core)
    far = (seq, lax.rem(head + 2, 4))
    far_twin = (seq, lax.rem(head + 3 - 2 * core, 4))

    def around(i):
        return lax.rem(seq + i, 64)

    def piece_of(device):
        return lax.div(device, 16) * 8 + lax.rem(lax.div(device, 2), 4) * 2 + lax.rem(device, 2)

    def near(o, sign):
        step = lax.div(o, 8)
        shift = step + 5 * lax.div(step, 2) - 6 * lax.div(step, 3) + 4 * core * lax.div(step, 3)
        xo = lax.rem(lax.div(o, 2), 4)
        nx = lax.rem(x + 4 + sign * xo, 4)
        nz = lax.rem(z + 8 + sign * shift, 8)
        ny = lax.rem(y + lax.rem(o, 2), 2)
        return nx * 16 + nz * 2 + ny

    barrier = pltpu.get_barrier_semaphore()

    def greet(i, carry):
        pl.semaphore_signal(barrier, inc=1, device_id=(around(i), head), device_id_type=MESH)
        return carry

    lax.fori_loop(1, 64, greet, 0)
    pl.semaphore_signal(barrier, inc=1, device_id=twin, device_id_type=MESH)
    pl.semaphore_signal(barrier, inc=1, device_id=far, device_id_type=MESH)
    pl.semaphore_signal(barrier, inc=1, device_id=far_twin, device_id_type=MESH)

    early = [
        pltpu.make_async_copy(src, dst, insem.at[n])
        for n, (src, dst) in enumerate(
            [(lat_hbm, lat_ref), (rope_hbm, rope_ref), (order_hbm, order_ref), (order_hbm, order_sm)]
        )
    ]
    for load in early:
        load.start()
    loads = [
        pltpu.make_async_copy(src, dst, insem.at[4 + n])
        for n, (src, dst) in enumerate(
            [(qn_hbm, qn), (qr_hbm, qr), (uk_hbm, uk), (uv_hbm, uv), (go_hbm, gout), (mask_hbm, mask_ref)]
        )
    ]
    for load in loads:
        load.start()

    for load in early:
        load.wait()

    lanes = lax.broadcasted_iota(jnp.int32, (128, PAD), 1)
    rope = jnp.concatenate([rope_ref[...].astype(F32), jnp.zeros((PAD - ROPE, 128), F32)], 0)
    keyf[0] = rope.T
    for b in range(2):
        keyf[b + 1] = lat_ref[:, pl.ds(pl.multiple_of(core * 256 + b * 128, 128), 128)].astype(F32)
    xbuf[...] = jnp.zeros_like(xbuf)
    for t in range(2):
        for q in range(2):
            for jb in range(3):
                xbuf[pl.ds((t * 2 + q) * 3 + jb, 32, stride=16), :] = keyf[
                    jb, pl.ds(t * GROUP + q, 32, stride=2), :
                ]
    send1[...] = xbuf[pl.ds(0, 512), :].astype(BF16).reshape(32, 16, 128)

    sub = lax.broadcasted_iota(jnp.int32, (8, 128), 0)
    cin = lax.broadcasted_iota(jnp.int32, (128, 128), 0)
    cout = lax.broadcasted_iota(jnp.int32, (128, 128), 1)
    reorder = jnp.where(cin == 2 * lax.rem(cout, 64) + lax.div(cout, 64), 1.0, 0.0).astype(BF16)
    plain = jnp.broadcast_to(order_ref[...].astype(F32).reshape(1, 128), (8, 128)).astype(BF16)
    row = dot_nn(plain, reorder)
    zero8 = jnp.zeros((8, 128), F32)

    def fill(n, carry):
        which = lax.div(n, 32)
        group = order_sm[2 * near(lax.rem(n, 32), 1) + which]
        hot = jnp.where(row == (sub + (group - (SPAN - 1))).astype(F32), 1.0, 0.0).astype(F32)
        upper = jnp.concatenate([hot, zero8], 1)
        lower = jnp.concatenate([zero8, hot], 1)
        onehot[pl.ds(pl.multiple_of(n * 16, 16), 16), :] = jnp.concatenate([upper, lower], 0).astype(BF16)
        return carry

    lax.fori_loop(0, 64, fill, 0)
    recvb[...] = jnp.zeros_like(recvb)
    pl.semaphore_wait(barrier, 66)

    pltpu.make_async_copy(send1.at[piece], recv1.at[seq], r1).start()

    def phase1(i, carry):
        dst = around(i)
        pltpu.make_async_remote_copy(
            src_ref=send1.at[piece_of(dst)], dst_ref=recv1.at[seq], send_sem=s1, recv_sem=r1,
            device_id=(dst, head), device_id_type=MESH,
        ).start()
        return carry

    lax.fori_loop(1, 64, phase1, 0)

    for load in loads:
        load.wait()

    def project(h, carry):
        cols = pl.ds(pl.multiple_of(h * NOPE, NOPE), NOPE)
        rows = pl.ds(pl.multiple_of(h * GROUP, GROUP), GROUP)
        ql = dot_nt(qn[:, cols], uk[:, cols]).astype(BF16)
        gl = dot_nt(gout[:, cols], uv[:, cols]).astype(BF16)
        for w in range(2):
            qfull[w, rows, pl.ds(PAD, LATENT)] = ql[w * GROUP:(w + 1) * GROUP]
            glow[w, rows, :] = gl[w * GROUP:(w + 1) * GROUP]
        return carry

    lax.fori_loop(0, HEAD_DEV, project, 0)

    pltpu.make_async_copy(recv1, recv1, r1).wait()
    xbuf[...] = recv1[...].reshape(1024, 128).astype(F32)
    for q in range(2):
        for t in range(2):
            for jb in range(3):
                gather2[(q * 2 + t) * 64:(q * 2 + t + 1) * 64, jb * 128:(jb + 1) * 128] = xbuf[
                    pl.ds((t * 2 + q) * 3 + jb, 64, stride=16), :
                ].astype(BF16)

    def half_of(ref, cr):
        return ref if cr == 0 else ref.at[:, pl.ds(128, 256)]

    def columns(cr):
        return pl.ds(0, 384) if cr == 0 else pl.ds(384, 256)

    def by_core(run):
        for cr in range(2):
            @pl.when(core == cr)
            def _():
                run(cr)

    for which in range(2):
        picked = dot_nn(onehot[which * 512:(which + 1) * 512, :], gather2[...])
        send2[which] = picked.astype(BF16).reshape(32, 16, 384)

        def send_windows(cr):
            pltpu.make_async_copy(
                half_of(send2.at[which, 0], cr), window.at[which, piece, :, columns(cr)], r2.at[which]
            ).start()

            def phase2(o, carry):
                pltpu.make_async_remote_copy(
                    src_ref=half_of(send2.at[which, o], cr), dst_ref=window.at[which, piece, :, columns(cr)],
                    send_sem=s2.at[which], recv_sem=r2.at[which],
                    device_id=(near(o, 1), head), device_id_type=MESH,
                ).start()
                return carry

            lax.fori_loop(1, 32, phase2, 0)

        by_core(send_windows)

    def rotary(m, carry):
        two = qr[:, pl.ds(pl.multiple_of(m * 128, 128), 128)].astype(F32)
        even = jnp.where(lanes < ROPE, two, 0.0).astype(BF16)
        odd = jnp.where(lanes < ROPE, pltpu.roll(two, ROPE, 1), 0.0).astype(BF16)
        for w in range(2):
            qfull[w, pl.ds(pl.multiple_of(m * 128, 128), GROUP), pl.ds(0, PAD)] = even[w * GROUP:(w + 1) * GROUP]
            qfull[w, pl.ds(pl.multiple_of(m * 128 + GROUP, GROUP), GROUP), pl.ds(0, PAD)] = odd[
                w * GROUP:(w + 1) * GROUP
            ]
        return carry

    lax.fori_loop(0, HEAD_DEV // 2, rotary, 0)

    col = lax.broadcasted_iota(jnp.int32, (GROUP, KEYS), 1)
    slot = lax.rem(col, SPAN)
    key_row = lax.div(col, SPAN)
    query_row = lax.broadcasted_iota(jnp.int32, (GROUP, KEYS), 0)
    for which in range(2):
        group = order_sm[2 * seq + which]
        seen = jnp.sum(mask_ref[pl.ds(group, 1), :], axis=1, keepdims=True)
        allowed = (slot >= SPAN - seen) & ((slot < SPAN - 1) | (key_row <= query_row))
        bias[which] = jnp.where(allowed, 0.0, -1e30).astype(F32)

    def cross_copy(src, dst, sem_s, sem_r):
        return pltpu.make_async_remote_copy(
            src_ref=src, dst_ref=dst, send_sem=sem_s, recv_sem=sem_r, device_id=twin, device_id_type=MESH
        )

    for which in range(2):
        onehot_t[which] = onehot[which * 512:(which + 1) * 512, :].T

    def share_window(which):
        def run(cr):
            ref = window.at[which, :, :, columns(cr)]
            pltpu.make_async_copy(ref, ref, r2.at[which]).wait()
            cross_copy(ref, ref, s2c.at[which], r2c.at[which]).start()

        by_core(run)

    def await_window(which):
        def run(cr):
            ref = window.at[which, :, :, columns(1 - cr)]
            pltpu.make_async_copy(ref, ref, r2c.at[which]).wait()

        by_core(run)

    def attend_from(which, first, last):
        def attend(n, carry):
            keys = window[which].reshape(KEYS, WIDTH)
            lat = keys[:, PAD:]
            parts = [pl.ds(pl.multiple_of(n * BLOCK + i * SUB, SUB), SUB) for i in range(BLOCK // SUB)]
            scores = [dot_nt(qfull[which, rows, :], keys) for rows in parts]
            grad_prob = [dot_nt(glow[which, rows, :], lat) for rows in parts]
            for i, rows in enumerate(parts):
                score = scores[i] * SCALE2
                score = (score.reshape(SUB // GROUP, GROUP, KEYS) + bias[which][None]).reshape(SUB, KEYS)
                top = jnp.max(score, axis=1, keepdims=True)
                weights = jnp.exp2(score - top)
                normed = weights * (1.0 / jnp.sum(weights, axis=1, keepdims=True))
                low = normed.astype(BF16)
                probs[rows, :] = low
                ol = dot_nn(low, lat).astype(BF16)
                prod = normed * grad_prob[i]
                delta = jnp.sum(prod, axis=1, keepdims=True)
                ds = (prod - normed * delta).astype(BF16)
                dscore[rows, :] = ds
                gq = (dot_nn(ds, keys) * SCALE).astype(BF16)
                first_head = n * (BLOCK // GROUP) + i * (SUB // GROUP)
                for j in range(SUB // GROUP):
                    part_rows = slice(j * GROUP, (j + 1) * GROUP)
                    olat[first_head + j, which * GROUP:(which + 1) * GROUP, :] = ol[part_rows]
                    gqlat[first_head + j, which * GROUP:(which + 1) * GROUP, :] = gq[part_rows, PAD:]
                for j in range(0, SUB // GROUP, 2):
                    two = jnp.concatenate(
                        [gq[j * GROUP:(j + 1) * GROUP, :ROPE], gq[(j + 1) * GROUP:(j + 2) * GROUP, :ROPE]], 1
                    )
                    gqr_v[
                        which * GROUP:(which + 1) * GROUP,
                        pl.ds(pl.multiple_of(n * BLOCK + i * SUB + j * ROPE, 128), 128),
                    ] = two
            return carry

        lax.fori_loop(first, last, attend, 0)

    def key_grads(which, h):
        krows = slice(h * 256, (h + 1) * 256)
        first = dot_tn(dscore[:, krows], qfull[which]) * SCALE
        second = dot_tn(probs[:, krows], glow[which])
        total = jnp.concatenate([first[:, :PAD], first[:, PAD:] + second], 1)
        dwin[which, h * 16:(h + 1) * 16] = total.reshape(16, 16, WIDTH)

    def share_grads(which, h):
        some = pl.ds(h * 16, 16)

        def run(cr):
            rest = columns(1 - cr)
            into = pl.ds(128, 256) if cr == 0 else pl.ds(0, 384)
            dsend[which, some, :, into] = dwin[which, some, :, rest].astype(BF16)
            cross_copy(
                dsend.at[which, some, :, into], dpair.at[which, some, :, into],
                s3c.at[2 * which + h], r3c.at[2 * which + h],
            ).start()

        by_core(run)

    def send_grads(which, h):
        some = pl.ds(h * 16, 16)

        def run(cr):
            into = pl.ds(0, 384) if cr == 0 else pl.ds(128, 256)
            ref = dpair.at[which, some, :, into]
            pltpu.make_async_copy(ref, ref, r3c.at[2 * which + h]).wait()
            dmine[which, some, :, into] = (
                dwin[which, some, :, columns(cr)] + dpair[which, some, :, into].astype(F32)
            ).astype(BF16)

            def phase4(i, carry):
                xo = lax.rem(x + 4 - (2 * h + lax.rem(lax.div(i, 2), 2)), 4)
                o = (3 - lax.div(i, 4)) * 8 + xo * 2 + lax.rem(i, 2)
                dst = near(o, -1)
                src_ref = half_of(dmine.at[which, piece_of(dst)], cr)
                dst_ref = half_of(recvb.at[which, o], cr)

                @pl.when(o == 0)
                def _():
                    pltpu.make_async_copy(src_ref, dst_ref, r4.at[which]).start()

                @pl.when(o != 0)
                def _():
                    pltpu.make_async_remote_copy(
                        src_ref=src_ref, dst_ref=dst_ref, send_sem=s4.at[which], recv_sem=r4.at[which],
                        device_id=(dst, head), device_id_type=MESH,
                    ).start()

                return carry

            lax.fori_loop(0, 16, phase4, 0)

        by_core(run)

    blocks = ROWS // BLOCK
    share_window(0)
    await_window(0)
    attend_from(0, 0, 1)
    share_window(1)
    attend_from(0, 1, blocks)
    for h in range(2):
        key_grads(0, h)
        share_grads(0, h)
    await_window(1)
    attend_from(1, 0, 1)
    for h in range(2):
        send_grads(0, h)
    attend_from(1, 1, blocks)
    for h in range(2):
        key_grads(1, h)
        share_grads(1, h)
    for h in range(2):
        send_grads(1, h)

    def unproject(h, carry):
        cols = pl.ds(pl.multiple_of(h * NOPE, NOPE), NOPE)
        out_v[:, cols] = dot_nn(olat[h], uv[:, cols]).astype(BF16)
        gqn_v[:, cols] = dot_nn(gqlat[h], uk[:, cols]).astype(BF16)
        return carry

    lax.fori_loop(0, HEAD_DEV, unproject, 0)
    stores = [
        pltpu.make_async_copy(src, dst, outsem.at[n])
        for n, (src, dst) in enumerate([(out_v, out_hbm), (gqn_v, gqn_hbm), (gqr_v, gqr_hbm)])
    ]
    for store in stores:
        store.start()

    total = jnp.zeros((256, 384), F32)
    for which in range(2):
        def await_grads(cr):
            ref = recvb.at[which] if cr == 0 else recvb.at[which, :, :, pl.ds(128, 256)]
            pltpu.make_async_copy(ref, ref, r4.at[which]).wait()

        by_core(await_grads)
        total = total + dot_nn(onehot_t[which], recvb[which].reshape(512, 384))
    for q in range(2):
        for t in range(2):
            for jb in range(3):
                xbuf[pl.ds((t * 2 + q) * 3 + jb, 64, stride=16), :] = total[
                    (q * 2 + t) * 64:(q * 2 + t + 1) * 64, jb * 128:(jb + 1) * 128
                ]
    send7[...] = xbuf[...].astype(BF16).reshape(64, 16, 128)

    pltpu.make_async_copy(send7.at[seq], recv7.at[plane, piece], r7).start()

    def phase7(i, carry):
        dst = around(i)
        pltpu.make_async_remote_copy(
            src_ref=send7.at[dst], dst_ref=recv7.at[plane, piece], send_sem=s7, recv_sem=r7,
            device_id=(dst, head), device_id_type=MESH,
        ).start()
        return carry

    lax.fori_loop(1, 64, phase7, 0)
    pltpu.make_async_copy(recv7, recv7, r7).wait()
    xbuf[pl.ds(0, 512), :] = (recv7[0].astype(F32) + recv7[1].astype(F32)).reshape(512, 128)
    for t in range(2):
        for q in range(2):
            for jb in range(3):
                keyf[jb, pl.ds(t * GROUP + q, 32, stride=2), :] = xbuf[
                    pl.ds((t * 2 + q) * 3 + jb, 32, stride=16), :
                ]
    home[pl.ds(head * 3, 3)] = keyf[...].astype(BF16)

    def send_home(cr):
        ref = home.at[pl.ds(head * 3 + cr, 3 - cr)]
        for dst in (far, far_twin, twin):
            pltpu.make_async_remote_copy(
                src_ref=ref, dst_ref=ref, send_sem=s9, recv_sem=r9, device_id=dst, device_id_type=MESH
            ).start()
        got = home.at[pl.ds(0, 7 + cr)]
        pltpu.make_async_copy(got, got, r9).wait()

    by_core(send_home)

    def both(block):
        return home[block].astype(F32) + home[block + 6].astype(F32)

    for b in range(4):
        glat_ref[:, b * 128:(b + 1) * 128] = both(b // 2 * 3 + b % 2 + 1).astype(BF16)
    grope_ref[...] = both(0).T[:ROPE].astype(BF16)

    def drain(ref, sem):
        pltpu.make_async_copy(ref, ref, sem).wait()

    drain(recv1.at[pl.ds(0, 63)], s1)
    drain(send7.at[pl.ds(0, 63)], s7)

    def drain_halves(cr):
        for which in range(2):
            own = pl.ds(0, 384) if cr == 0 else pl.ds(128, 256)
            rest = pl.ds(128, 256) if cr == 0 else pl.ds(0, 384)
            drain(send2.at[which, pl.ds(0, 31), :, own], s2.at[which])
            drain(dmine.at[which, pl.ds(0, 31), :, own], s4.at[which])
            drain(window.at[which, :, :, columns(cr)], s2c.at[which])
            for h in range(2):
                drain(dsend.at[which, pl.ds(h * 16, 16), :, rest], s3c.at[2 * which + h])

    by_core(drain_halves)

    def drain_home(cr):
        ref = home.at[pl.ds(0, 3 * (3 - cr))]
        drain(ref, s9)

    by_core(drain_home)
    for store in stores:
        store.wait()


def copy_kernel(*refs):
    count = (len(refs) - 2) // 3
    srcs, dsts, held = refs[:count], refs[count:2 * count], refs[2 * count:3 * count]
    insem, outsem = refs[3 * count:]
    reads = [pltpu.make_async_copy(srcs[n], held[n], insem.at[n]) for n in range(count)]
    writes = [pltpu.make_async_copy(held[n], dsts[n], outsem.at[n]) for n in range(count)]
    for read in reads:
        read.start()
    for read, write in zip(reads, writes):
        read.wait()
        write.start()
    for write in writes:
        write.wait()


def local(
    query_nope, query_rope, latent, key_rope, up_key, up_value, grad_out, group_order, tile_mask
):
    vmem = pl.BlockSpec(memory_space=pltpu.VMEM)
    hbm = pl.BlockSpec(memory_space=pl.ANY)
    dma = pltpu.SemaphoreType.DMA
    scratch = [
        pltpu.VMEM((128, LATENT), BF16),
        pltpu.VMEM((ROPE, 128), BF16),
        pltpu.SMEM((128,), jnp.int32),
        pltpu.VMEM((128,), jnp.int32),
        pltpu.VMEM((128, 2048), BF16),
        pltpu.VMEM((128, 1024), BF16),
        pltpu.VMEM((LATENT, 2048), BF16),
        pltpu.VMEM((LATENT, 2048), BF16),
        pltpu.VMEM((128, 2048), BF16),
        pltpu.VMEM((128, 128), jnp.int32),
        pltpu.VMEM((128, 2048), BF16),
        pltpu.VMEM((128, 2048), BF16),
        pltpu.VMEM((128, 1024), BF16),
        pltpu.VMEM((3, 128, 128), F32),
        pltpu.VMEM((1024, 128), F32),
        pltpu.VMEM((32, 16, 128), BF16),
        pltpu.VMEM((64, 16, 128), BF16),
        pltpu.VMEM((256, 384), BF16),
        pltpu.VMEM((1024, 256), BF16),
        pltpu.VMEM((2, 32, 16, 384), BF16),
        pltpu.VMEM((2, 32, 16, WIDTH), BF16),
        pltpu.VMEM((2, ROWS, WIDTH), BF16),
        pltpu.VMEM((2, ROWS, LATENT), BF16),
        pltpu.VMEM((HEAD_DEV, 128, LATENT), BF16),
        pltpu.VMEM((HEAD_DEV, 128, LATENT), BF16),
        pltpu.VMEM((ROWS, KEYS), BF16),
        pltpu.VMEM((ROWS, KEYS), BF16),
        pltpu.VMEM((2, GROUP, KEYS), F32),
        pltpu.VMEM((2, 32, 16, WIDTH), F32),
        pltpu.VMEM((2, 32, 16, 384), BF16),
        pltpu.VMEM((2, 32, 16, 384), BF16),
        pltpu.VMEM((2, 32, 16, 384), BF16),
        pltpu.VMEM((2, 32, 16, 384), BF16),
        pltpu.VMEM((2, 256, 512), BF16),
        pltpu.VMEM((64, 16, 128), BF16),
        pltpu.VMEM((2, 32, 16, 128), BF16),
        pltpu.VMEM((12, 128, 128), BF16),
        dma((10,)), dma((3,)),
        dma, dma,
        dma((2,)), dma((2,)), dma((2,)), dma((2,)),
        dma((4,)), dma((4,)),
        dma((2,)), dma((2,)),
        dma, dma, dma, dma,
    ]
    shapes = (
        jax.ShapeDtypeStruct((128, 2048), BF16),
        jax.ShapeDtypeStruct((128, 2048), BF16),
        jax.ShapeDtypeStruct((128, 1024), BF16),
        jax.ShapeDtypeStruct((128, LATENT), BF16),
        jax.ShapeDtypeStruct((ROPE, 128), BF16),
    )
    results = pl.pallas_call(
        kernel,
        out_shape=shapes,
        in_specs=[hbm] * 9,
        out_specs=(hbm, hbm, hbm, vmem, vmem),
        scratch_shapes=scratch,
        compiler_params=pltpu.CompilerParams(
            collective_id=0, has_side_effects=True, vmem_limit_bytes=56 << 20
        ),
    )(
        query_nope, query_rope, latent, key_rope.T, up_key, up_value, grad_out,
        group_order, tile_mask,
    )
    out, gqn, gqr, glat, grope = pl.pallas_call(
        copy_kernel,
        out_shape=shapes,
        in_specs=[hbm] * 5,
        out_specs=(hbm,) * 5,
        scratch_shapes=[pltpu.VMEM(a.shape, a.dtype) for a in shapes] + [dma((5,)), dma((5,))],
    )(*results)
    return out, gqn, gqr, glat, grope.T


def solution(mesh):
    placed = (
        P("seq", "head"),
        P("seq", "head"),
        P("seq", None),
        P("seq", None),
        P(None, "head"),
        P(None, "head"),
        P("seq", "head"),
        P(),
        P(),
    )
    return jax.shard_map(
        local,
        mesh=mesh,
        in_specs=placed,
        out_specs=(
            P("seq", "head"),
            P("seq", "head"),
            P("seq", "head"),
            P("seq", None),
            P("seq", None),
        ),
        check_vma=False,
    )
```
